256 devices in a mesh: dp: 8 (over z), mp: 16 (over y, x), section: 2 (over core).
Axes of the slice: x: 4, y: 4, z: 8, core: 2. Of those that a mesh axis runs over, the one named last changes fastest.
Arguments:
- acts: bfloat16 [2, 4096, 6144], P('section', 'dp', 'mp'), may hold values from -6 to 6
- halting: int32 [2, 4096], P('section', 'dp'), may hold values from 0 to 2, as said below
- norm_gain: float32 [2, 6144], P('section'), may hold values from 0.1 to 1.9
- qkv_weight: bfloat16 [2, 6144, 12288], P('section', None, 'mp'), may hold values from -0.078125 to 0.078125
- qk_gain: float32 [2, 2, 32, 128], P('section', None, 'mp'), may hold values from 0.5 to 11, as said below
- out_weight: bfloat16 [2, 4096, 6144], P('section', None, 'mp'), may hold values from -0.09375 to 0.09375
Outputs:
- mixed: bfloat16 [2, 4096, 6144], P('section', 'dp', 'mp')
The draws below stay inside these ranges and needn't reach their ends.
Inputs may be any that keep to these rules, and one draw needn't show every extreme that they name: `halting`: A token of segment s takes part in that segment's layer exactly when its value is greater than s. Among the 512 tokens of one device at one segment at most 384 are live, exactly 384 on some device of every segment, and at least 128. `qk_gain`: Positive.
All inputs are finite; a program needn't handle non-finite values.
Results may differ from the reference program's by a relative error of at most 0.012.
Values may be sent and summed in bfloat16 or wider, within the bound.
A program may use at most 128 MiB of HBM per device.

```python
import math
import jax
import jax.numpy as jnp
from jax import lax

D = 6144
HEAD = 128
GROUP = 4
TOK_DEV = 512
HEADS = 32
IMAGES = 2
TOKENS = 4096
N_DP = 8
N_SECTION = 2


def draw_halting(key, part):
    key = jax.random.fold_in(key, 11)
    first, second, third, fourth = jax.random.split(key, 4)
    most = 3 * TOK_DEV // 4
    counts = jax.random.randint(first, (N_SECTION, N_DP), TOK_DEV // 4, most + 1)
    full_at = jax.random.randint(second, (N_SECTION, 1), 0, N_DP)
    counts = jnp.where(jnp.arange(N_DP)[None, :] == full_at, most, counts)
    block_keys = jax.random.split(third, N_SECTION * N_DP)
    order = jax.vmap(lambda k: jax.random.permutation(k, TOK_DEV))(block_keys)
    order = order.reshape(N_SECTION, N_DP, TOK_DEV)
    live = order < counts[:, :, None]
    segment = jnp.arange(N_SECTION)[:, None, None]
    noise = jax.random.randint(fourth, (N_SECTION, N_DP, TOK_DEV), 0, 1 << 20)
    live_value = segment + 1 + noise % (N_SECTION - segment)
    dead_value = noise % (segment + 1)
    return jnp.where(live, live_value, dead_value).reshape(N_SECTION, TOKENS).astype(jnp.int32)


def draw_qk_gain(key, part):
    key = jax.random.fold_in(key, 23)
    first, second = jax.random.split(key, 2)
    level = jax.random.uniform(first, (N_SECTION, 2, HEADS, 1), jnp.float32, jnp.log(1.2), jnp.log(2.4))
    detail = jax.random.uniform(second, (N_SECTION, 2, HEADS, HEAD), jnp.float32, 0.8, 1.2)
    return (jnp.exp(level) * detail).astype(jnp.float32)


def block_scale(key, dims, cuts, least, top_value):
    loudness, own = 1.0, jax.random.fold_in(key, 6)
    for axis_at, shards_of in cuts:
        heights = jnp.exp(jax.random.uniform(jax.random.fold_in(own, axis_at), (shards_of,), jnp.float32, least / len(cuts), top_value / len(cuts)))
        loudness = loudness * jnp.repeat(heights, dims[axis_at] // shards_of).reshape([-1 if axis == axis_at else 1 for axis in range(len(dims))])
    return loudness


def bell_draw(stream_key, extent, width, reach, shards=(), kind=jnp.bfloat16):
    values = jax.random.normal(stream_key, extent, jnp.float32) * width
    if len(shards) > 0:
        values = block_scale(stream_key, extent, shards, -0.22, 0.18) * values
    return jnp.clip(values, min=-reach, max=reach).astype(kind)


def setup_inputs(seed: int = 0) -> dict:
    splits = jax.random.split(jax.random.key(seed), 7)
    return {
        "acts": bell_draw(splits[0], (N_SECTION, TOKENS, D), 1.0, 6.0, ((0, 2), (1, 8), (2, 16))),
        "halting": draw_halting(jax.random.fold_in(splits[6], 71), 0),
        "norm_gain": jnp.clip(1.0 + 0.18 * jax.random.normal(splits[2], (N_SECTION, D), jnp.float32), 0.1, 1.9),
        "qkv_weight": bell_draw(splits[3], (N_SECTION, D, 3 * HEADS * HEAD), D ** -0.5, 0.078125, ((0, 2), (2, 16))),
        "qk_gain": draw_qk_gain(jax.random.fold_in(splits[6], 71), 0),
        "out_weight": bell_draw(splits[5], (N_SECTION, HEADS * HEAD, D), (HEADS * HEAD) ** -0.5, 0.09375, ((0, 2), (2, 16))),
    }


def row_norm(values, gain):
    mean = lax.optimization_barrier(jnp.mean(values, axis=-1, keepdims=True))
    centred = values - mean
    spread = lax.optimization_barrier(jnp.mean(centred * centred, axis=-1, keepdims=True))
    return centred * lax.rsqrt(spread + 1e-06) * gain

def attend(query, keys, values, flags):
    scores = jnp.einsum('qhe,khe->hqk', query.astype(jnp.float32), keys.astype(jnp.float32)) / math.sqrt(query.shape[-1])
    scores = jnp.where(flags[None, None, :], scores, -jnp.inf)
    top = lax.optimization_barrier(jnp.max(scores, axis=-1, keepdims=True))
    weights = jnp.exp(scores - top)
    total = lax.optimization_barrier(jnp.sum(weights, axis=-1))
    rounded = weights.astype(jnp.bfloat16)
    summed = jnp.einsum('hqk,khe->qhe', rounded.astype(jnp.float32), values.astype(jnp.float32))
    return (summed / jnp.transpose(total)[:, :, None]).astype(jnp.bfloat16)

def layer(x, halt, gain, wqkv, gains, wout, segment):
    live = halt > segment
    normed = row_norm(x.astype(jnp.float32), gain).astype(jnp.bfloat16)
    qkv = jnp.dot(normed, wqkv, preferred_element_type=jnp.float32).reshape(TOKENS, HEADS, 3, HEAD)
    query = row_norm(qkv[:, :, 0], gains[0]).astype(jnp.bfloat16)
    keys = row_norm(qkv[:, :, 1], gains[1]).astype(jnp.bfloat16)
    values = qkv[:, :, 2].astype(jnp.bfloat16)

    def shaped(array):
        return array.reshape((IMAGES, GROUP * TOK_DEV) + array.shape[1:])

    def per_image(items):
        return attend(items[0], items[1], items[2], items[3])
    heads_out = lax.map(per_image, (shaped(query), shaped(keys), shaped(values), shaped(live)))
    heads_out = heads_out.reshape(TOKENS, HEADS * HEAD)
    projected = jnp.dot(heads_out, wout, preferred_element_type=jnp.float32)
    wide = x.astype(jnp.float32)
    return jnp.where(live[:, None], wide + projected, wide).astype(jnp.bfloat16)

def reference(acts, halting, norm_gain, qkv_weight, qk_gain, out_weight):
    results = [layer(acts[s], halting[s], norm_gain[s], qkv_weight[s], qk_gain[s], out_weight[s], s) for s in range(N_SECTION)]
    return jnp.stack([results[(s - 1) % N_SECTION] for s in range(N_SECTION)])
```

```python
import functools
import math

import jax
import jax.numpy as jnp
from jax import lax
from jax.experimental import pallas as pl
from jax.experimental.pallas import tpu as pltpu
from jax.sharding import PartitionSpec as P

MESH = pl.DeviceIdType.MESH
HEAD = 128
GROUP = 4
SIDE = 4
TOK = 512
LIVE = 384
FEAT = 384
HEADS_HERE = 2
WIDE = HEADS_HERE * HEAD
COLS = 3 * WIDE
ROWS = 128
CHUNKS = LIVE // ROWS
HALF = ROWS // 2
QUARTER = HALF // 2
SCALE = math.log2(math.e) / math.sqrt(HEAD)
F32 = jnp.float32
BF16 = jnp.bfloat16


class Gather:
    def __init__(self, buf, width, send, recv, x, y):
        self.buf, self.width, self.send, self.recv = buf, width, send, recv
        self.at = (y, x)
        self.started = []

    def ring(self, axis, by):
        return lax.rem(self.at[axis] + by + SIDE, SIDE)

    def device(self, axis, by):
        y, x = self.at
        if axis == 0:
            y = self.ring(0, by)
        else:
            x = self.ring(1, by)
        return {"mp": y * SIDE + x}

    def block(self, c, first, a, b, row, rows):
        y, x = (b, a) if first == 1 else (a, b)
        lanes = pl.ds(pl.multiple_of(x * self.width, 128), self.width)
        return self.buf.at[c, y, pl.ds(row, rows), lanes]

    def slab(self, c, first, b, row, low, count):
        if first == 1:
            return self.buf.at[c, b, pl.ds(row, HALF), pl.ds(low * self.width, count * self.width)]
        lanes = pl.ds(pl.multiple_of(b * self.width, 128), self.width)
        return self.buf.at[c, pl.ds(low, count), pl.ds(row, HALF), lanes]

    def copy(self, ref, c, first, k, device):
        at = (c * 2 + first) * 8 + k
        return pltpu.make_async_remote_copy(
            src_ref=ref,
            dst_ref=ref,
            send_sem=self.send.at[at],
            recv_sem=self.recv.at[at],
            device_id=device,
            device_id_type=MESH,
        )

    def step(self, c, stage):
        for first in (1, 0):
            self.half_step(c, stage, first)

    def half_step(self, c, stage, first):
        second = 1 - first
        row = 0 if first == 1 else HALF
        a, b = self.at[first], self.at[second]
        up, down = self.device(first, 1), self.device(first, -1)
        out, back = self.device(second, 1), self.device(second, -1)
        if stage >= 1:
            got = {
                1: lambda: (
                    self.block(c, first, self.ring(first, -1), b, row, HALF),
                    self.block(c, first, self.ring(first, 1), b, row, HALF),
                ),
                2: lambda: (
                    self.block(c, first, self.ring(first, 2), b, row, QUARTER),
                    self.block(c, first, self.ring(first, 2), b, row + QUARTER, QUARTER),
                ),
                3: lambda: (
                    self.slab(c, first, self.ring(second, -1), row, 0, SIDE),
                    self.slab(c, first, self.ring(second, 1), row, 0, SIDE),
                ),
                4: lambda: (
                    self.slab(c, first, self.ring(second, 2), row, 0, 2),
                    self.slab(c, first, self.ring(second, 2), row, 2, 2),
                ),
            }[stage]()
            for side in (0, 1):
                self.copy(got[side], c, first, (stage - 1) * 2 + side, up).wait_recv()
        if stage == 0:
            own = self.block(c, first, a, b, row, HALF)
            sends = ((own, up), (own, down))
        elif stage == 1:
            sends = (
                (self.block(c, first, self.ring(first, -1), b, row, QUARTER), up),
                (self.block(c, first, self.ring(first, 1), b, row + QUARTER, QUARTER), down),
            )
        elif stage == 2:
            own = self.slab(c, first, b, row, 0, SIDE)
            sends = ((own, out), (own, back))
        elif stage == 3:
            sends = (
                (self.slab(c, first, self.ring(second, -1), row, 0, 2), out),
                (self.slab(c, first, self.ring(second, 1), row, 2, 2), back),
            )
        else:
            sends = ()
        for side, (ref, device) in enumerate(sends):
            copy = self.copy(ref, c, first, stage * 2 + side, device)
            copy.start()
            self.started.append(copy)

    def finish(self):
        for copy in self.started:
            copy.wait_send()


class Line:
    def __init__(self, kv, send, recv, z):
        self.kv, self.send, self.recv, self.z = kv, send, recv, z
        self.p = lax.rem(z, GROUP)

    def copy(self, c, j, way):
        at = (c * 3 + j) * 2 + (0 if way > 0 else 1)
        ref = self.kv.at[self.p - way * j, c]
        return pltpu.make_async_remote_copy(
            src_ref=ref,
            dst_ref=ref,
            send_sem=self.send.at[at],
            recv_sem=self.recv.at[at],
            device_id={"dp": self.z + way},
            device_id_type=MESH,
        )

    def arriving(self, c, j, way):
        at = (c * 3 + j) * 2 + (0 if way > 0 else 1)
        ref = self.kv.at[self.p - way * (j + 1), c]
        return pltpu.make_async_remote_copy(
            src_ref=ref,
            dst_ref=ref,
            send_sem=self.send.at[at],
            recv_sem=self.recv.at[at],
            device_id={"dp": self.z - way},
            device_id_type=MESH,
        )

    def has(self, way, j):
        return self.p >= j if way > 0 else self.p + j < GROUP

    def sends(self, way, j):
        more = self.p < GROUP - 1 if way > 0 else self.p > 0
        return jnp.logical_and(more, self.has(way, j))

    def step(self, c, j):
        for way in (1, -1):
            if j > 0:
                pl.when(self.has(way, j))(lambda: self.arriving(c, j - 1, way).wait_recv())
            if j < 3:
                pl.when(self.sends(way, j))(lambda: self.copy(c, j, way).start())

    def finish(self):
        for c in range(CHUNKS):
            for j in range(3):
                for way in (1, -1):
                    pl.when(self.sends(way, j))(lambda: self.copy(c, j, way).wait_send())


def normed(values, gain):
    mean = jnp.mean(values, axis=-1, keepdims=True)
    centred = values - mean
    spread = jnp.mean(centred * centred, axis=-1, keepdims=True)
    return centred * lax.rsqrt(spread + 1e-06) * gain


def kernel(
    x_ref, halt_ref, gain_ref, qk_ref, w_hbm, wo_hbm, out_ref,
    w, wo, xg, xn, acc, kv, query, counts, flags, hg, pick, place, rest, result, outgoing,
    w_sem, a_send, a_recv, c_send, c_recv, z_send, z_recv, n_send, n_recv, o_send, o_recv,
):
    z = lax.axis_index("dp")
    m = lax.axis_index("mp")
    s = lax.axis_index("section")
    x, y = lax.rem(m, SIDE), m // SIDE
    p = lax.rem(z, GROUP)
    base = z - p

    barrier = pltpu.get_barrier_semaphore()
    peers = [{"dp": base + lax.rem(p + j, GROUP)} for j in (1, 2, 3)]
    neighbours = [
        {"mp": y * SIDE + lax.rem(x + 1, SIDE)},
        {"mp": y * SIDE + lax.rem(x + SIDE - 1, SIDE)},
        {"mp": lax.rem(y + 1, SIDE) * SIDE + x},
        {"mp": lax.rem(y + SIDE - 1, SIDE) * SIDE + x},
        {"section": 1 - s},
    ]
    for device in neighbours + peers:
        pl.semaphore_signal(barrier, inc=1, device_id=device, device_id_type=MESH)

    load_w = pltpu.make_async_copy(w_hbm, w, w_sem.at[0])
    load_wo = pltpu.make_async_copy(wo_hbm, wo, w_sem.at[1])
    load_w.start()
    load_wo.start()

    live = jnp.where(halt_ref[...] > s, 1.0, 0.0)
    before = lax.broadcasted_iota(jnp.int32, (TOK, TOK), 0) < lax.broadcasted_iota(jnp.int32, (TOK, TOK), 1)
    rank = jnp.dot(
        jnp.broadcast_to(live, (16, TOK)).astype(BF16),
        jnp.where(before, 1.0, 0.0).astype(BF16),
        preferred_element_type=F32,
    )[0:1]
    count = jnp.sum(live, axis=-1, keepdims=True)
    rank = jnp.where(live > 0.5, rank, -1.0)
    row = lax.broadcasted_iota(jnp.int32, (LIVE, TOK), 0).astype(F32)
    chosen = jnp.broadcast_to(rank, (LIVE, TOK)) == jnp.minimum(row, jnp.broadcast_to(count, (LIVE, TOK)) - 1.0)
    first = jnp.where(chosen, 1.0, 0.0)
    pick[...] = jnp.where(row < jnp.broadcast_to(count, (LIVE, TOK)), first, 0.0)
    compact = jnp.dot(first.astype(BF16), x_ref[...], preferred_element_type=F32).astype(BF16)
    own = pl.ds(pl.multiple_of(x * FEAT, 128), FEAT)
    for c in range(CHUNKS):
        xg[c, y, :, own] = compact[c * ROWS : (c + 1) * ROWS]
    counts[p] = jnp.broadcast_to(count, (8, 128))

    pl.semaphore_wait(barrier, 8)

    ga = Gather(xg, FEAT, a_send, a_recv, x, y)
    gc = Gather(hg, WIDE, c_send, c_recv, x, y)
    line = Line(kv, z_send, z_recv, z)

    def count_copy(j, ref, device):
        return pltpu.make_async_remote_copy(
            src_ref=ref,
            dst_ref=ref,
            send_sem=n_send.at[j],
            recv_sem=n_recv.at[j],
            device_id=device,
            device_id_type=MESH,
        )

    def project(c):
        def rows(i, _):
            at = pl.ds(pl.multiple_of(i * 16, 16), 16)
            total = jnp.zeros((16, 1), F32)
            for b in range(SIDE):
                total += jnp.sum(xg[c, b, at, :].astype(F32), axis=-1, keepdims=True)
            mean = total * (1.0 / (16 * FEAT))
            square = jnp.zeros((16, 1), F32)
            for b in range(SIDE):
                centred = xg[c, b, at, :].astype(F32) - mean
                square += jnp.sum(centred * centred, axis=-1, keepdims=True)
            scale = lax.rsqrt(square * (1.0 / (16 * FEAT)) + 1e-06)
            for b in range(SIDE):
                lanes = slice(b * SIDE * FEAT, (b + 1) * SIDE * FEAT)
                centred = xg[c, b, at, :].astype(F32) - mean
                xn[b, at, :] = (centred * scale * gain_ref[:, lanes]).astype(BF16)
            return 0

        lax.fori_loop(0, ROWS // 16, rows, 0)
        if c == 0:
            load_w.wait()
        acc[...] = jnp.zeros_like(acc)

        def part(b, _):
            depth = pl.ds(pl.multiple_of(b * SIDE * FEAT, 128), SIDE * FEAT)
            acc[...] += jnp.dot(xn[b], w[depth, :], preferred_element_type=F32)
            return 0

        lax.fori_loop(0, SIDE, part, 0)
        real = lax.broadcasted_iota(jnp.int32, (ROWS, HEAD), 0).astype(F32) + c * ROWS < jnp.broadcast_to(count, (ROWS, HEAD))
        for h in range(HEADS_HERE):
            col = h * 3 * HEAD
            query[c, h] = normed(acc[:, col : col + HEAD], qk_ref[0, h : h + 1, :]).astype(BF16)
            kv[p, c, :, h * HEAD : (h + 1) * HEAD] = normed(
                acc[:, col + HEAD : col + 2 * HEAD], qk_ref[1, h : h + 1, :]
            ).astype(BF16)
            kv[p, c, :, WIDE + h * HEAD : WIDE + (h + 1) * HEAD] = jnp.where(
                real, acc[:, col + 2 * HEAD : col + 3 * HEAD], 0.0
            ).astype(BF16)

    def attend(c):
        for h in range(HEADS_HERE):
            keys = kv[:, :, :, h * HEAD : (h + 1) * HEAD].reshape(GROUP * LIVE, HEAD)
            values = kv[:, :, :, WIDE + h * HEAD : WIDE + (h + 1) * HEAD].reshape(GROUP * LIVE, HEAD)
            scores = (
                lax.dot_general(query[c, h], keys, (((1,), (1,)), ((), ())), preferred_element_type=F32) * SCALE
            )
            top = jnp.max(scores, axis=-1, keepdims=True)
            weights = jnp.exp2(scores - top).astype(BF16)
            summed = jnp.dot(
                weights, jnp.concatenate([values, flags[...]], axis=1), preferred_element_type=F32
            )
            lanes = pl.ds(pl.multiple_of(x * WIDE + h * HEAD, 128), HEAD)
            hg[c, y, :, lanes] = (summed[:, :HEAD] / summed[:, HEAD:]).astype(BF16)

    def close(c):
        if c == 0:
            load_wo.wait()
        total = jnp.zeros((ROWS, FEAT), F32)
        for b in range(SIDE):
            total += jnp.dot(
                hg[c, b], wo[b * SIDE * WIDE : (b + 1) * SIDE * WIDE, :], preferred_element_type=F32
            )
        mine = xg[c, y, :, own].astype(F32)
        result[c * ROWS : (c + 1) * ROWS, :] = (mine + total).astype(BF16)
        low, high = c * ROWS, (c + 1) * ROWS if c < CHUNKS - 1 else TOK
        known = (c + 1) * ROWS
        placed = jnp.dot(place[low:high, :known], result[:known, :], preferred_element_type=F32)
        outgoing[low:high, :] = (rest[low:high, :].astype(F32) + placed).astype(BF16)
        copy = pltpu.make_async_remote_copy(
            src_ref=outgoing.at[pl.ds(low, high - low)],
            dst_ref=out_ref.at[pl.ds(low, high - low)],
            send_sem=o_send.at[c],
            recv_sem=o_recv.at[c],
            device_id={"section": 1 - s},
            device_id_type=MESH,
        )
        copy.start()
        return copy

    ga.step(0, 0)
    for j in (1, 2, 3):
        count_copy(j - 1, counts.at[p], peers[j - 1]).start()
    ga.step(1, 0)
    ga.step(0, 1)
    ga.step(0, 2)
    ga.step(1, 1)
    ga.step(2, 0)

    place[...] = jnp.transpose(pick[...]).astype(BF16)
    rest[...] = (
        x_ref[...].astype(F32) - jnp.dot(place[...], compact, preferred_element_type=F32)
    ).astype(BF16)
    for j in (1, 2, 3):
        count_copy(j - 1, counts.at[lax.rem(p + GROUP - j, GROUP)], peers[j - 1]).wait_recv()
    place_of = lax.broadcasted_iota(jnp.int32, (LIVE, HEAD), 0).astype(F32)
    for q in range(GROUP):
        flags[q * LIVE : (q + 1) * LIVE, :] = jnp.where(
            place_of < jnp.broadcast_to(counts[q, 0:1, :], (LIVE, HEAD)), 1.0, 0.0
        ).astype(BF16)

    ga.step(0, 3)
    ga.step(1, 2)
    ga.step(2, 1)
    ga.step(0, 4)
    project(0)
    line.step(0, 0)
    ga.step(1, 3)
    ga.step(2, 2)
    line.step(0, 1)
    ga.step(1, 4)
    line.step(0, 2)
    project(1)
    line.step(1, 0)
    ga.step(2, 3)
    line.step(0, 3)
    line.step(1, 1)
    ga.step(2, 4)
    project(2)
    line.step(2, 0)
    line.step(1, 2)
    line.step(2, 1)
    line.step(1, 3)
    line.step(2, 2)
    line.step(2, 3)

    attend(0)
    gc.step(0, 0)
    attend(1)
    gc.step(1, 0)
    gc.step(0, 1)
    attend(2)
    gc.step(0, 2)
    gc.step(1, 1)
    gc.step(2, 0)
    gc.step(0, 3)
    gc.step(1, 2)
    gc.step(2, 1)
    gc.step(0, 4)
    copies = [close(0)]
    gc.step(1, 3)
    gc.step(2, 2)
    gc.step(1, 4)
    copies.append(close(1))
    gc.step(2, 3)
    gc.step(2, 4)
    copies.append(close(2))

    for j in (1, 2, 3):
        count_copy(j - 1, counts.at[p], peers[j - 1]).wait_send()
    ga.finish()
    gc.finish()
    line.finish()
    for copy in copies:
        copy.wait()


def body(acts, halting, norm_gain, qkv_weight, qk_gain, out_weight):
    vmem = pl.BlockSpec(memory_space=pltpu.VMEM)
    anywhere = pl.BlockSpec(memory_space=pl.ANY)
    out = pl.pallas_call(
        kernel,
        out_shape=jax.ShapeDtypeStruct((TOK, FEAT), BF16),
        in_specs=[vmem, vmem, vmem, vmem, anywhere, anywhere],
        out_specs=anywhere,
        scratch_shapes=[
            pltpu.VMEM((16 * FEAT, COLS), BF16),
            pltpu.VMEM((16 * WIDE, FEAT), BF16),
            pltpu.VMEM((CHUNKS, SIDE, ROWS, SIDE * FEAT), BF16),
            pltpu.VMEM((SIDE, ROWS, SIDE * FEAT), BF16),
            pltpu.VMEM((ROWS, COLS), F32),
            pltpu.VMEM((GROUP, CHUNKS, ROWS, 2 * WIDE), BF16),
            pltpu.VMEM((CHUNKS, HEADS_HERE, ROWS, HEAD), BF16),
            pltpu.VMEM((GROUP, 8, 128), F32),
            pltpu.VMEM((GROUP * LIVE, HEAD), BF16),
            pltpu.VMEM((CHUNKS, SIDE, ROWS, SIDE * WIDE), BF16),
            pltpu.VMEM((LIVE, TOK), F32),
            pltpu.VMEM((TOK, LIVE), BF16),
            pltpu.VMEM((TOK, FEAT), BF16),
            pltpu.VMEM((LIVE, FEAT), BF16),
            pltpu.VMEM((TOK, FEAT), BF16),
            pltpu.SemaphoreType.DMA((2,)),
            pltpu.SemaphoreType.DMA((CHUNKS * 16,)),
            pltpu.SemaphoreType.DMA((CHUNKS * 16,)),
            pltpu.SemaphoreType.DMA((CHUNKS * 16,)),
            pltpu.SemaphoreType.DMA((CHUNKS * 16,)),
            pltpu.SemaphoreType.DMA((CHUNKS * 6,)),
            pltpu.SemaphoreType.DMA((CHUNKS * 6,)),
            pltpu.SemaphoreType.DMA((3,)),
            pltpu.SemaphoreType.DMA((3,)),
            pltpu.SemaphoreType.DMA((CHUNKS,)),
            pltpu.SemaphoreType.DMA((CHUNKS,)),
        ],
        compiler_params=pltpu.CompilerParams(
            collective_id=0, has_side_effects=True, vmem_limit_bytes=56 * 1024 * 1024
        ),
    )(acts[0], halting, norm_gain, qk_gain[0], qkv_weight[0], out_weight[0])
    return out[None]


def solution(mesh):
    return jax.shard_map(
        body,
        mesh=mesh,
        in_specs=(
            P("section", "dp", "mp"),
            P("section", "dp"),
            P("section", None),
            P("section", None, "mp"),
            P("section", None, "mp", None),
            P("section", None, "mp"),
        ),
        out_specs=P("section", "dp", "mp"),
        check_vma=False,
    )
```

```python
import functools
import math

import jax
import jax.numpy as jnp
from jax import lax
from jax.experimental import pallas as pl
from jax.experimental.pallas import tpu as pltpu
from jax.sharding import PartitionSpec as P

MESH = pl.DeviceIdType.MESH
HEAD = 128
GROUP = 4
SIDE = 4
TOK = 512
LIVE = 384
FEAT = 384
HEADS_HERE = 2
WIDE = HEADS_HERE * HEAD
COLS = 3 * WIDE
ROWS = 128
CHUNKS = LIVE // ROWS
SCALE = math.log2(math.e) / math.sqrt(HEAD)
F32 = jnp.float32
BF16 = jnp.bfloat16


PIECES_A = (
    (0, 32, 1, 0), (32, 32, 0, 0), (64, 64, 1, 0), (128, 64, 0, 0), (192, 64, 1, 0), (256, 64, 0, 0),
    (320, 32, 1, 0), (352, 32, 0, 0),
)
PIECES_C = ((0, 64, 1, 1), (64, 64, 0, 1), (128, 64, 1, 1), (192, 64, 0, 1), (256, 64, 1, 1), (320, 64, 0, 1))
PARTS = ((0, 64), (64, 128), (192, 128), (320, 64))

ORDER = (
    ("gate",), ("a", 0, 0), ("a", 1, 0), ("a", 2, 0), ("a", 3, 0), ("greet",), ("a", 0, 1), ("a", 1, 1), ("a", 4, 0), ("a", 5, 0),
    ("a", 2, 1), ("a", 3, 1), ("a", 6, 0), ("a", 7, 0), ("a", 4, 1), ("a", 5, 1), ("prepare",), ("a", 0, 2), ("a", 1, 2),
    ("project", 0), ("z", 0, 0), ("a", 6, 1), ("a", 7, 1), ("open",), ("a", 2, 2), ("a", 3, 2), ("project", 1), ("z", 1, 0),
    ("z", 0, 1), ("a", 4, 2), ("a", 5, 2), ("project", 2), ("z", 2, 0), ("z", 0, 2), ("z", 1, 1), ("a", 6, 2), ("a", 7, 2),
    ("project", 3), ("z", 3, 0), ("z", 0, 3), ("z", 1, 2), ("z", 2, 1), ("z", 1, 3), ("z", 3, 1), ("z", 2, 2), ("z", 2, 3), ("z", 3, 2), ("z", 3, 3),
    ("attend", 0), ("c", 0, 0), ("c", 1, 0), ("attend", 1), ("c", 2, 0), ("c", 3, 0), ("attend", 2), ("c", 4, 0), ("c", 5, 0),
    ("c", 0, 1), ("c", 1, 1), ("c", 2, 1), ("c", 3, 1), ("c", 4, 1), ("c", 5, 1),
    ("c", 0, 2), ("c", 1, 2), ("c", 2, 2), ("c", 3, 2), ("c", 4, 2), ("c", 5, 2), ("c", 0, 3), ("c", 1, 3), ("close", 0),
    ("c", 2, 3), ("c", 3, 3), ("close", 1), ("c", 4, 3), ("c", 5, 3), ("close", 2),
)


class Gather:
    def __init__(self, buf, pieces, send, recv, x, y):
        self.buf, self.pieces, self.send, self.recv = buf, pieces, send, recv
        self.at = (y, x)
        self.started = []

    def ring(self, axis, by):
        return lax.rem(self.at[axis] + by + SIDE, SIDE)

    def device(self, axis, by):
        y, x = self.at
        if axis == 0:
            y = self.ring(0, by)
        else:
            x = self.ring(1, by)
        return {"mp": y * SIDE + x}

    def copy(self, ref, n, k, device):
        at = n * 8 + k
        return pltpu.make_async_remote_copy(
            src_ref=ref,
            dst_ref=ref,
            send_sem=self.send.at[at],
            recv_sem=self.recv.at[at],
            device_id=device,
            device_id_type=MESH,
        )

    def plan(self, n):
        row, rows, first, way = self.pieces[n]
        second = 1 - first
        half = rows // 2

        def block(by, low=0, count=rows):
            a = self.ring(first, by)
            y, x = (self.at[0], a) if first == 1 else (a, self.at[1])
            return lambda: self.buf.at[y, x, pl.ds(row + low, count), :]

        def slab(by, low=0, count=SIDE):
            b = self.ring(second, by)
            if first == 1:
                return lambda: self.buf.at[b, pl.ds(low, count), pl.ds(row, rows), :]
            return lambda: self.buf.at[pl.ds(low, count), b, pl.ds(row, rows), :]

        whole = (1, -1, 2)
        if way < 2:
            sends = [[(k, block(0), first, d) for k, d in enumerate(whole)]]
            arrivals = [[(k, block(-d)) for k, d in enumerate(whole)]]
        else:
            sends = [
                [(0, block(0), first, 1), (1, block(0), first, -1)],
                [(2, block(-1, 0, half), first, 1), (3, block(1, half, half), first, -1)],
            ]
            arrivals = [[(0, block(-1)), (1, block(1))], [(2, block(2, 0, half)), (3, block(2, half, half))]]
        if way < 1:
            sends += [[(4 + k, slab(0), second, d) for k, d in enumerate(whole)]]
            arrivals += [[(4 + k, slab(-d)) for k, d in enumerate(whole)]]
        else:
            sends += [
                [(4, slab(0), second, 1), (5, slab(0), second, -1)],
                [(6, slab(-1, 0, 2), second, 1), (7, slab(1, 2, 2), second, -1)],
            ]
            arrivals += [[(4, slab(-1)), (5, slab(1))], [(6, slab(2, 0, 2)), (7, slab(2, 2, 2))]]
        return sends, arrivals

    def step(self, n, stage):
        sends, arrivals = self.plan(n)
        if stage > 0:
            for k, ref in arrivals[stage - 1]:
                self.copy(ref(), n, k, self.device(0, 1)).wait_recv()
        if stage < len(sends):
            for k, ref, axis, by in sends[stage]:
                copy = self.copy(ref(), n, k, self.device(axis, by))
                copy.start()
                self.started.append(copy)

    def finish(self):
        for copy in self.started:
            copy.wait_send()


class Line:
    def __init__(self, kv, send, recv, z):
        self.kv, self.send, self.recv, self.z = kv, send, recv, z
        self.p = lax.rem(z, GROUP)
        self.started = []

    def copy(self, c, j, way):
        at = (c * 3 + j) * 2 + (0 if way > 0 else 1)
        ref = self.kv.at[self.p - way * j, pl.ds(*PARTS[c])]
        return pltpu.make_async_remote_copy(
            src_ref=ref,
            dst_ref=ref,
            send_sem=self.send.at[at],
            recv_sem=self.recv.at[at],
            device_id={"dp": self.z + way},
            device_id_type=MESH,
        )

    def arriving(self, c, j, way):
        at = (c * 3 + j) * 2 + (0 if way > 0 else 1)
        ref = self.kv.at[self.p - way * (j + 1), pl.ds(*PARTS[c])]
        return pltpu.make_async_remote_copy(
            src_ref=ref,
            dst_ref=ref,
            send_sem=self.send.at[at],
            recv_sem=self.recv.at[at],
            device_id={"dp": self.z - way},
            device_id_type=MESH,
        )

    def has(self, way, j):
        return self.p >= j if way > 0 else self.p + j < GROUP

    def sends(self, way, j):
        more = self.p < GROUP - 1 if way > 0 else self.p > 0
        return jnp.logical_and(more, self.has(way, j))

    def step(self, c, j):
        if j < 3:
            self.started.append((c, j))
        for way in (1, -1):
            if j > 0:
                pl.when(self.has(way, j))(lambda: self.arriving(c, j - 1, way).wait_recv())
            if j < 3:
                pl.when(self.sends(way, j))(lambda: self.copy(c, j, way).start())

    def finish(self):
        for c, j in self.started:
            for way in (1, -1):
                pl.when(self.sends(way, j))(lambda: self.copy(c, j, way).wait_send())


def normed(values, gain):
    mean = jnp.mean(values, axis=-1, keepdims=True)
    centred = values - mean
    spread = jnp.mean(centred * centred, axis=-1, keepdims=True)
    return centred * lax.rsqrt(spread + 1e-06) * gain


def kernel(
    x_ref, halt_ref, gain_ref, qk_ref, w_hbm, wo_hbm, out_ref,
    w, wo, xg, xn, acc, kv, query, counts, flags, hg, pick, place, rest, result, outgoing,
    w_sem, a_send, a_recv, c_send, c_recv, z_send, z_recv, n_send, n_recv, o_send, o_recv, turn,
):
    z = lax.axis_index("dp")
    m = lax.axis_index("mp")
    s = lax.axis_index("section")
    x, y = lax.rem(m, SIDE), m // SIDE
    p = lax.rem(z, GROUP)
    base = z - p

    barrier = pltpu.get_barrier_semaphore()
    peers = [{"dp": base + lax.rem(p + j, GROUP)} for j in (1, 2, 3)]
    neighbours = [
        {"mp": y * SIDE + lax.rem(x + 1, SIDE)},
        {"mp": y * SIDE + lax.rem(x + SIDE - 1, SIDE)},
        {"mp": y * SIDE + lax.rem(x + 2, SIDE)},
        {"mp": lax.rem(y + 1, SIDE) * SIDE + x},
        {"mp": lax.rem(y + 2, SIDE) * SIDE + x},
        {"mp": lax.rem(y + SIDE - 1, SIDE) * SIDE + x},
        {"section": 1 - s},
    ]
    for device in neighbours + peers:
        pl.semaphore_signal(barrier, inc=1, device_id=device, device_id_type=MESH)

    load_w = pltpu.make_async_copy(w_hbm, w, w_sem.at[0])
    load_wo = pltpu.make_async_copy(wo_hbm, wo, w_sem.at[1])
    load_w.start()
    load_wo.start()

    live = jnp.where(halt_ref[...] > s, 1.0, 0.0)
    before = lax.broadcasted_iota(jnp.int32, (TOK, TOK), 0) < lax.broadcasted_iota(jnp.int32, (TOK, TOK), 1)
    rank = jnp.dot(
        jnp.broadcast_to(live, (16, TOK)).astype(BF16),
        jnp.where(before, 1.0, 0.0).astype(BF16),
        preferred_element_type=F32,
    )[0:1]
    count = jnp.sum(live, axis=-1, keepdims=True)
    rank = jnp.where(live > 0.5, rank, -1.0)
    row = lax.broadcasted_iota(jnp.int32, (LIVE, TOK), 0).astype(F32)
    chosen = jnp.broadcast_to(rank, (LIVE, TOK)) == jnp.minimum(row, jnp.broadcast_to(count, (LIVE, TOK)) - 1.0)
    first = jnp.where(chosen, 1.0, 0.0)
    pick[...] = jnp.where(row < jnp.broadcast_to(count, (LIVE, TOK)), first, 0.0)
    compact = jnp.dot(first.astype(BF16), x_ref[...], preferred_element_type=F32).astype(BF16)
    xg[y, x] = compact
    counts[p] = jnp.broadcast_to(count, (8, 128))

    pl.semaphore_wait(barrier, 10)

    ga = Gather(xg, PIECES_A, a_send, a_recv, x, y)
    gc = Gather(hg, PIECES_C, c_send, c_recv, x, y)
    line = Line(kv, z_send, z_recv, z)

    def count_copy(j, ref, device):
        return pltpu.make_async_remote_copy(
            src_ref=ref,
            dst_ref=ref,
            send_sem=n_send.at[j],
            recv_sem=n_recv.at[j],
            device_id=device,
            device_id_type=MESH,
        )

    def project(c):
        low, rows = PARTS[c]
        for at in range(low, low + rows, 64):
            at = slice(at, at + 64)
            total = jnp.zeros((64, 1), F32)
            for b in range(16):
                total += jnp.sum(xg[b // SIDE, b % SIDE, at].astype(F32), axis=-1, keepdims=True)
            mean = total * (1.0 / (16 * FEAT))
            square = jnp.zeros((64, 1), F32)
            for b in range(16):
                centred = xg[b // SIDE, b % SIDE, at].astype(F32) - mean
                square += jnp.sum(centred * centred, axis=-1, keepdims=True)
            scale = lax.rsqrt(square * (1.0 / (16 * FEAT)) + 1e-06)
            for b in range(16):
                lanes = slice(b * FEAT, (b + 1) * FEAT)
                centred = xg[b // SIDE, b % SIDE, at].astype(F32) - mean
                xn[at.start - low : at.stop - low, lanes] = (centred * scale * gain_ref[:, lanes]).astype(BF16)
        if c == 0:
            load_w.wait()
        total = jnp.zeros((rows, COLS), F32)
        for b in range(8):
            depth = slice(b * 2 * FEAT, (b + 1) * 2 * FEAT)
            total += jnp.dot(xn[:rows, depth], w[depth, :], preferred_element_type=F32)
        acc[:rows] = total
        at = slice(low, low + rows)
        real = lax.broadcasted_iota(jnp.int32, (rows, HEAD), 0).astype(F32) + low < jnp.broadcast_to(count, (rows, HEAD))
        for h in range(HEADS_HERE):
            col = h * 3 * HEAD
            query[h, at] = normed(acc[:rows, col : col + HEAD], qk_ref[0, h : h + 1, :]).astype(BF16)
            kv[p, at, h * HEAD : (h + 1) * HEAD] = normed(
                acc[:rows, col + HEAD : col + 2 * HEAD], qk_ref[1, h : h + 1, :]
            ).astype(BF16)
            kv[p, at, WIDE + h * HEAD : WIDE + (h + 1) * HEAD] = jnp.where(
                real, acc[:rows, col + 2 * HEAD : col + 3 * HEAD], 0.0
            ).astype(BF16)

    def attend(c):
        for h in range(HEADS_HERE):
            keys = kv[:, :, h * HEAD : (h + 1) * HEAD].reshape(GROUP * LIVE, HEAD)
            values = kv[:, :, WIDE + h * HEAD : WIDE + (h + 1) * HEAD].reshape(GROUP * LIVE, HEAD)
            scores = (
                lax.dot_general(query[h, c * ROWS : (c + 1) * ROWS], keys, (((1,), (1,)), ((), ())), preferred_element_type=F32) * SCALE
            )
            top = jnp.max(scores, axis=-1, keepdims=True)
            weights = jnp.exp2(scores - top).astype(BF16)
            summed = jnp.dot(
                weights, jnp.concatenate([values, flags[...]], axis=1), preferred_element_type=F32
            )
            heads = (summed[:, :HEAD] / summed[:, HEAD:]).astype(BF16)
            hg[y, x, c * ROWS : (c + 1) * ROWS, h * HEAD : (h + 1) * HEAD] = heads

    def close(c):
        if c == 0:
            load_wo.wait()
        total = jnp.zeros((ROWS, FEAT), F32)
        for b in range(SIDE):
            heads = jnp.concatenate([hg[b, i, c * ROWS : (c + 1) * ROWS] for i in range(SIDE)], axis=1)
            total += jnp.dot(heads, wo[b * SIDE * WIDE : (b + 1) * SIDE * WIDE, :], preferred_element_type=F32)
        mine = xg[y, x, c * ROWS : (c + 1) * ROWS].astype(F32)
        result[c * ROWS : (c + 1) * ROWS, :] = (mine + total).astype(BF16)
        low, high = c * ROWS, (c + 1) * ROWS if c < CHUNKS - 1 else TOK
        known = (c + 1) * ROWS
        placed = jnp.dot(place[low:high, :known], result[:known, :], preferred_element_type=F32)
        outgoing[low:high, :] = (rest[low:high, :].astype(F32) + placed).astype(BF16)
        copy = pltpu.make_async_remote_copy(
            src_ref=outgoing.at[pl.ds(low, high - low)],
            dst_ref=out_ref.at[pl.ds(low, high - low)],
            send_sem=o_send.at[c],
            recv_sem=o_recv.at[c],
            device_id={"section": 1 - s},
            device_id_type=MESH,
        )
        copy.start()
        return copy

    copies = []

    def greet():
        for j in (1, 2, 3):
            count_copy(j - 1, counts.at[p], peers[j - 1]).start()

    def prepare():
        place[...] = jnp.transpose(pick[...]).astype(BF16)
        rest[...] = (
            x_ref[...].astype(F32) - jnp.dot(place[...], compact, preferred_element_type=F32)
        ).astype(BF16)
        for j in (1, 2, 3):
            count_copy(j - 1, counts.at[lax.rem(p + GROUP - j, GROUP)], peers[j - 1]).wait_recv()
        place_of = lax.broadcasted_iota(jnp.int32, (LIVE, HEAD), 0).astype(F32)
        for q in range(GROUP):
            flags[q * LIVE : (q + 1) * LIVE, :] = jnp.where(
                place_of < jnp.broadcast_to(counts[q, 0:1, :], (LIVE, HEAD)), 1.0, 0.0
            ).astype(BF16)

    def gate():
        pl.when(s == 1)(lambda: pl.semaphore_wait(turn, 1))

    def open_gate():
        @pl.when(s == 0)
        def _():
            pl.semaphore_signal(turn, inc=1, device_id={"section": 1 - s}, device_id_type=MESH)

    steps = {
        "a": ga.step, "c": gc.step, "z": line.step, "project": project, "attend": attend,
        "close": lambda c: copies.append(close(c)), "greet": greet, "prepare": prepare,
        "gate": gate, "open": open_gate,
    }
    for name, *at in ORDER:
        steps[name](*at)

    for j in (1, 2, 3):
        count_copy(j - 1, counts.at[p], peers[j - 1]).wait_send()
    ga.finish()
    gc.finish()
    line.finish()
    for copy in copies:
        copy.wait()


def body(acts, halting, norm_gain, qkv_weight, qk_gain, out_weight):
    vmem = pl.BlockSpec(memory_space=pltpu.VMEM)
    anywhere = pl.BlockSpec(memory_space=pl.ANY)
    out = pl.pallas_call(
        kernel,
        out_shape=jax.ShapeDtypeStruct((TOK, FEAT), BF16),
        in_specs=[vmem, vmem, vmem, vmem, anywhere, anywhere],
        out_specs=anywhere,
        scratch_shapes=[
            pltpu.VMEM((16 * FEAT, COLS), BF16),
            pltpu.VMEM((16 * WIDE, FEAT), BF16),
            pltpu.VMEM((SIDE, SIDE, LIVE, FEAT), BF16),
            pltpu.VMEM((ROWS, 16 * FEAT), BF16),
            pltpu.VMEM((ROWS, COLS), F32),
            pltpu.VMEM((GROUP, LIVE, 2 * WIDE), BF16),
            pltpu.VMEM((HEADS_HERE, LIVE, HEAD), BF16),
            pltpu.VMEM((GROUP, 8, 128), F32),
            pltpu.VMEM((GROUP * LIVE, HEAD), BF16),
            pltpu.VMEM((SIDE, SIDE, LIVE, WIDE), BF16),
            pltpu.VMEM((LIVE, TOK), F32),
            pltpu.VMEM((TOK, LIVE), BF16),
            pltpu.VMEM((TOK, FEAT), BF16),
            pltpu.VMEM((LIVE, FEAT), BF16),
            pltpu.VMEM((TOK, FEAT), BF16),
            pltpu.SemaphoreType.DMA((2,)),
            pltpu.SemaphoreType.DMA((len(PIECES_A) * 8,)),
            pltpu.SemaphoreType.DMA((len(PIECES_A) * 8,)),
            pltpu.SemaphoreType.DMA((len(PIECES_C) * 8,)),
            pltpu.SemaphoreType.DMA((len(PIECES_C) * 8,)),
            pltpu.SemaphoreType.DMA((len(PARTS) * 6,)),
            pltpu.SemaphoreType.DMA((len(PARTS) * 6,)),
            pltpu.SemaphoreType.DMA((3,)),
            pltpu.SemaphoreType.DMA((3,)),
            pltpu.SemaphoreType.DMA((CHUNKS,)),
            pltpu.SemaphoreType.DMA((CHUNKS,)),
            pltpu.SemaphoreType.REGULAR,
        ],
        compiler_params=pltpu.CompilerParams(
            collective_id=0, has_side_effects=True, vmem_limit_bytes=56 * 1024 * 1024
        ),
    )(acts[0], halting, norm_gain, qk_gain[0], qkv_weight[0], out_weight[0])
    return out[None]


def solution(mesh):
    return jax.shard_map(
        body,
        mesh=mesh,
        in_specs=(
            P("section", "dp", "mp"),
            P("section", "dp"),
            P("section", None),
            P("section", None, "mp"),
            P("section", None, "mp", None),
            P("section", None, "mp"),
        ),
        out_specs=P("section", "dp", "mp"),
        check_vma=False,
    )
```

```python
import functools
import math

import jax
import jax.numpy as jnp
from jax import lax
from jax.experimental import pallas as pl
from jax.experimental.pallas import tpu as pltpu
from jax.sharding import PartitionSpec as P

MESH = pl.DeviceIdType.MESH
HEAD = 128
GROUP = 4
SIDE = 4
TOK = 512
LIVE = 384
FEAT = 384
HEADS_HERE = 2
WIDE = HEADS_HERE * HEAD
COLS = 3 * WIDE
ROWS = 128
CHUNKS = LIVE // ROWS
SCALE = math.log2(math.e) / math.sqrt(HEAD)
F32 = jnp.float32
BF16 = jnp.bfloat16


PIECES_A = ((0, 32, 1, 0), (32, 32, 0, 0), (64, 64, 1, 0), (128, 64, 0, 0), (192, 64, 1, 0), (256, 64, 0, 0), (320, 32, 1, 0), (352, 32, 0, 0))
PIECES_C = ((0, 64, 1, 1), (64, 64, 0, 1), (128, 64, 1, 1), (192, 64, 0, 1), (256, 64, 1, 1), (320, 64, 0, 1))
PARTS = ((0, 64), (64, 128), (192, 128), (320, 64))

DIRECT = (3,)

ORDER = (
    ("a", 0, 0), ("a", 0, 1), ("a", 1, 0), ("a", 1, 1), ("gate",), ("a", 2, 0), ("a", 2, 1), ("a", 3, 0), ("a", 3, 1),
    ("greet",), ("a", 0, 2), ("a", 1, 2), ("a", 4, 0), ("a", 4, 1), ("a", 5, 0), ("a", 5, 1), ("a", 2, 2),
    ("a", 3, 2), ("a", 6, 0), ("a", 6, 1), ("a", 7, 0), ("a", 7, 1), ("a", 4, 2), ("a", 5, 2), ("prepare",),
    ("a", 0, 3), ("a", 1, 3), ("project", 0), ("z", 0, 0), ("a", 6, 2), ("a", 7, 2), ("open",), ("a", 2, 3),
    ("a", 3, 3), ("project", 1), ("z", 1, 0), ("z", 0, 1), ("a", 4, 3), ("a", 5, 3), ("project", 2), ("z", 2, 0),
    ("z", 1, 1), ("a", 6, 3), ("a", 7, 3), ("project", 3), ("z", 3, 0), ("z", 2, 1), ("z", 0, 2), ("z", 1, 2),
    ("z", 2, 2), ("z", 3, 2), ("attend", 0), ("c", 0, 0), ("c", 0, 1), ("c", 1, 0), ("c", 1, 1), ("attend", 1),
    ("c", 2, 0), ("c", 2, 1), ("c", 3, 0), ("c", 3, 1), ("attend", 2), ("c", 4, 0), ("c", 4, 1), ("c", 5, 0),
    ("c", 5, 1), ("c", 0, 2), ("c", 1, 2), ("c", 2, 2), ("c", 3, 2), ("c", 4, 2), ("c", 5, 2), ("c", 0, 3),
    ("c", 1, 3), ("c", 2, 3), ("c", 3, 3), ("c", 4, 3), ("c", 5, 3), ("c", 0, 4), ("c", 1, 4), ("close", 0),
    ("c", 2, 4), ("c", 3, 4), ("close", 1), ("c", 4, 4), ("c", 5, 4), ("close", 2),
)


class Gather:
    def __init__(self, buf, pieces, send, recv, x, y):
        self.buf, self.pieces, self.send, self.recv = buf, pieces, send, recv
        self.at = (y, x)
        self.started = []

    def device(self, axis, by):
        y, x = self.at
        if axis == 0:
            y = lax.rem(y + by + SIDE, SIDE)
        else:
            x = lax.rem(x + by + SIDE, SIDE)
        return {"mp": y * SIDE + x}

    def copy(self, n, k, src, dst, device):
        at = n * 9 + k
        return pltpu.make_async_remote_copy(
            src_ref=src,
            dst_ref=dst,
            send_sem=self.send.at[at],
            recv_sem=self.recv.at[at],
            device_id=device,
            device_id_type=MESH,
        )

    def plan(self, n):
        row, rows, first, way = self.pieces[n]
        whole = ((0, 1), (1, -1), (2, 2))
        sends = [[(k, (0, 1), 0, first, d) for k, d in whole]]
        if way == 0:
            sends += [[(3 + k, (0, 1), 0, 1 - first, d) for k, d in whole]]
            sends += [[(6 + k, (1, 3), 0, 1 - first, d) for k, d in whole]]
            waits = ((), (), (0,), (1, 2))
        else:
            sends += [[(3 + k, (0, 1), 0, 1 - first, d) for k, d in whole[:2]]]
            sends += [[(5 + k, (1, 3), 0, 1 - first, d) for k, d in whole[:2]]]
            sends += [[(7, (0, 2), -1, 1 - first, 1), (8, (2, 2), 1, 1 - first, -1)]]
            waits = ((), (), (0,), (1, 2), (3,))
        return sends, waits

    def ref(self, n, low, count, second):
        row, rows, first, _ = self.pieces[n]
        second = second % SIDE
        if count == 1:
            y, x = (second, low % SIDE) if first == 1 else (low % SIDE, second)
            return self.buf.at[y, x, pl.ds(row, rows), :]
        if first == 1:
            return self.buf.at[second, pl.ds(low, count), pl.ds(row, rows), :]
        return self.buf.at[pl.ds(low, count), second, pl.ds(row, rows), :]

    def ends(self, n, at, second, axis, by):
        low, count = at
        src = self.ref(n, low, count, second)
        if axis == self.pieces[n][2]:
            return src, self.ref(n, low - by, count, second)
        return src, self.ref(n, low, count, second - by)

    def step(self, n, stage):
        sends, waits = self.plan(n)
        for before in waits[stage]:
            for k, at, second, axis, by in sends[before]:
                _, dst = self.ends(n, at, second, axis, by)
                self.copy(n, k, dst, dst, self.device(axis, by)).wait_recv()
        if stage < len(sends):
            for k, at, second, axis, by in sends[stage]:
                copy = self.copy(n, k, *self.ends(n, at, second, axis, by), self.device(axis, by))
                copy.start()
                self.started.append(copy)

    def finish(self):
        for copy in self.started:
            copy.wait_send()


class Line:
    def __init__(self, kv, send, recv, z):
        self.kv, self.send, self.recv, self.z = kv, send, recv, z
        self.p = lax.rem(z, GROUP)
        self.started = []

    def copy(self, c, d, way, owner, device):
        at = (c * 3 + d - 1) * 2 + (0 if way > 0 else 1)
        ref = self.kv.at[owner, pl.ds(*PARTS[c])]
        return pltpu.make_async_remote_copy(
            src_ref=ref,
            dst_ref=ref,
            send_sem=self.send.at[at],
            recv_sem=self.recv.at[at],
            device_id={"dp": device},
            device_id_type=MESH,
        )

    def reaches(self, d, way):
        return self.p < GROUP - d if way > 0 else self.p >= d

    def comes(self, d, way):
        return self.p >= d if way > 0 else self.p < GROUP - d

    def passes(self, way):
        return self.p == (2 if way > 0 else 1)

    def own(self, c, d, way):
        return self.copy(c, d, way, self.p, self.z + way * d)

    def passed(self, c, way):
        return self.copy(c, 3, way, self.p - way * 2, self.z + way)

    def arrival(self, c, d, way):
        return self.copy(c, d, way, self.p - way * d, self.z - way)

    def far(self, c):
        return (1, 2, 3) if c in DIRECT else (1, 2)

    def step(self, c, stage):
        for d in (1, 2, 3):
            for way in (1, -1):
                if stage == 0 and d in self.far(c):
                    pl.when(self.reaches(d, way))(lambda: self.own(c, d, way).start())
                if stage == 1 and d == 3:

                    @pl.when(self.passes(way))
                    def _():
                        self.arrival(c, 2, way).wait_recv()
                        self.passed(c, way).start()

                if stage == 2:
                    here = self.comes(d, way)
                    if d == 2 and c not in DIRECT:
                        here = jnp.logical_and(here, jnp.logical_not(self.passes(way)))
                    pl.when(here)(lambda: self.arrival(c, d, way).wait_recv())
        if stage == 0:
            self.started.append(c)

    def finish(self):
        for c in self.started:
            for way in (1, -1):
                for d in self.far(c):
                    pl.when(self.reaches(d, way))(lambda: self.own(c, d, way).wait_send())
                if c not in DIRECT:
                    pl.when(self.passes(way))(lambda: self.passed(c, way).wait_send())


def normed(values, gain):
    mean = jnp.mean(values, axis=-1, keepdims=True)
    centred = values - mean
    spread = jnp.mean(centred * centred, axis=-1, keepdims=True)
    return centred * lax.rsqrt(spread + 1e-06) * gain


def kernel(
    x_ref, halt_ref, gain_ref, qk_ref, w_hbm, wo_hbm, out_ref,
    w, wo, xg, xn, acc, kv, query, counts, flags, hg, pick, place, rest, result, outgoing,
    w_sem, a_send, a_recv, c_send, c_recv, z_send, z_recv, n_send, n_recv, o_send, o_recv, turn,
):
    z = lax.axis_index("dp")
    m = lax.axis_index("mp")
    s = lax.axis_index("section")
    x, y = lax.rem(m, SIDE), m // SIDE
    p = lax.rem(z, GROUP)
    base = z - p

    barrier = pltpu.get_barrier_semaphore()
    peers = [{"dp": base + lax.rem(p + j, GROUP)} for j in (1, 2, 3)]
    neighbours = [
        {"mp": y * SIDE + lax.rem(x + 1, SIDE)},
        {"mp": y * SIDE + lax.rem(x + SIDE - 1, SIDE)},
        {"mp": y * SIDE + lax.rem(x + 2, SIDE)},
        {"mp": lax.rem(y + 1, SIDE) * SIDE + x},
        {"mp": lax.rem(y + 2, SIDE) * SIDE + x},
        {"mp": lax.rem(y + SIDE - 1, SIDE) * SIDE + x},
        {"section": 1 - s},
    ]
    for device in neighbours + peers:
        pl.semaphore_signal(barrier, inc=1, device_id=device, device_id_type=MESH)

    load_w = pltpu.make_async_copy(w_hbm, w, w_sem.at[0])
    load_wo = pltpu.make_async_copy(wo_hbm, wo, w_sem.at[1])
    load_w.start()
    load_wo.start()

    live = jnp.where(halt_ref[...] > s, 1.0, 0.0)
    before = lax.broadcasted_iota(jnp.int32, (TOK, TOK), 0) < lax.broadcasted_iota(jnp.int32, (TOK, TOK), 1)
    rank = jnp.dot(
        jnp.broadcast_to(live, (16, TOK)).astype(BF16),
        jnp.where(before, 1.0, 0.0).astype(BF16),
        preferred_element_type=F32,
    )[0:1]
    count = jnp.sum(live, axis=-1, keepdims=True)
    rank = jnp.where(live > 0.5, rank, -1.0)
    row = lax.broadcasted_iota(jnp.int32, (LIVE, TOK), 0).astype(F32)
    chosen = jnp.broadcast_to(rank, (LIVE, TOK)) == jnp.minimum(row, jnp.broadcast_to(count, (LIVE, TOK)) - 1.0)
    first = jnp.where(chosen, 1.0, 0.0)
    pick[...] = jnp.where(row < jnp.broadcast_to(count, (LIVE, TOK)), first, 0.0)
    compact = jnp.dot(first.astype(BF16), x_ref[...], preferred_element_type=F32).astype(BF16)
    xg[0, 0] = compact
    counts[p] = jnp.broadcast_to(count, (8, 128))

    pl.semaphore_wait(barrier, 10)

    def from_here(b):
        return lax.rem(b // SIDE - y + SIDE, SIDE), lax.rem(b % SIDE - x + SIDE, SIDE)

    ga = Gather(xg, PIECES_A, a_send, a_recv, x, y)
    gc = Gather(hg, PIECES_C, c_send, c_recv, x, y)
    line = Line(kv, z_send, z_recv, z)

    def count_copy(j, ref, device):
        return pltpu.make_async_remote_copy(
            src_ref=ref,
            dst_ref=ref,
            send_sem=n_send.at[j],
            recv_sem=n_recv.at[j],
            device_id=device,
            device_id_type=MESH,
        )

    def project(c):
        low, rows = PARTS[c]
        for at in range(low, low + rows, 64):
            at = slice(at, at + 64)
            total = jnp.zeros((64, 1), F32)
            for b in range(16):
                total += jnp.sum(xg[*from_here(b), at].astype(F32), axis=-1, keepdims=True)
            mean = total * (1.0 / (16 * FEAT))
            square = jnp.zeros((64, 1), F32)
            for b in range(16):
                centred = xg[*from_here(b), at].astype(F32) - mean
                square += jnp.sum(centred * centred, axis=-1, keepdims=True)
            scale = lax.rsqrt(square * (1.0 / (16 * FEAT)) + 1e-06)
            for b in range(16):
                lanes = slice(b * FEAT, (b + 1) * FEAT)
                centred = xg[*from_here(b), at].astype(F32) - mean
                xn[at.start - low : at.stop - low, lanes] = (centred * scale * gain_ref[:, lanes]).astype(BF16)
        if c == 0:
            load_w.wait()
        total = jnp.zeros((rows, COLS), F32)
        for b in range(8):
            depth = slice(b * 2 * FEAT, (b + 1) * 2 * FEAT)
            total += jnp.dot(xn[:rows, depth], w[depth, :], preferred_element_type=F32)
        acc[:rows] = total
        at = slice(low, low + rows)
        real = lax.broadcasted_iota(jnp.int32, (rows, HEAD), 0).astype(F32) + low < jnp.broadcast_to(count, (rows, HEAD))
        for h in range(HEADS_HERE):
            col = h * 3 * HEAD
            query[h, at] = normed(acc[:rows, col : col + HEAD], qk_ref[0, h : h + 1, :]).astype(BF16)
            kv[p, at, h * HEAD : (h + 1) * HEAD] = normed(
                acc[:rows, col + HEAD : col + 2 * HEAD], qk_ref[1, h : h + 1, :]
            ).astype(BF16)
            kv[p, at, WIDE + h * HEAD : WIDE + (h + 1) * HEAD] = jnp.where(
                real, acc[:rows, col + 2 * HEAD : col + 3 * HEAD], 0.0
            ).astype(BF16)

    def attend(c):
        for h in range(HEADS_HERE):
            keys = kv[:, :, h * HEAD : (h + 1) * HEAD].reshape(GROUP * LIVE, HEAD)
            values = kv[:, :, WIDE + h * HEAD : WIDE + (h + 1) * HEAD].reshape(GROUP * LIVE, HEAD)
            scores = (
                lax.dot_general(query[h, c * ROWS : (c + 1) * ROWS], keys, (((1,), (1,)), ((), ())), preferred_element_type=F32) * SCALE
            )
            top = jnp.max(scores, axis=-1, keepdims=True)
            weights = jnp.exp2(scores - top).astype(BF16)
            summed = jnp.dot(
                weights, jnp.concatenate([values, flags[...]], axis=1), preferred_element_type=F32
            )
            heads = (summed[:, :HEAD] / summed[:, HEAD:]).astype(BF16)
            hg[0, 0, c * ROWS : (c + 1) * ROWS, h * HEAD : (h + 1) * HEAD] = heads

    def close(c):
        if c == 0:
            load_wo.wait()
        total = jnp.zeros((ROWS, FEAT), F32)
        for b in range(SIDE):
            heads = jnp.concatenate(
                [hg[*from_here(b * SIDE + i), c * ROWS : (c + 1) * ROWS] for i in range(SIDE)], axis=1
            )
            total += jnp.dot(heads, wo[b * SIDE * WIDE : (b + 1) * SIDE * WIDE, :], preferred_element_type=F32)
        mine = xg[0, 0, c * ROWS : (c + 1) * ROWS].astype(F32)
        result[c * ROWS : (c + 1) * ROWS, :] = (mine + total).astype(BF16)
        low, high = c * ROWS, (c + 1) * ROWS if c < CHUNKS - 1 else TOK
        known = (c + 1) * ROWS
        placed = jnp.dot(place[low:high, :known], result[:known, :], preferred_element_type=F32)
        outgoing[low:high, :] = (rest[low:high, :].astype(F32) + placed).astype(BF16)
        copy = pltpu.make_async_remote_copy(
            src_ref=outgoing.at[pl.ds(low, high - low)],
            dst_ref=out_ref.at[pl.ds(low, high - low)],
            send_sem=o_send.at[c],
            recv_sem=o_recv.at[c],
            device_id={"section": 1 - s},
            device_id_type=MESH,
        )
        copy.start()
        return copy

    copies = []

    def greet():
        for j in (1, 2, 3):
            count_copy(j - 1, counts.at[p], peers[j - 1]).start()

    def prepare():
        place[...] = jnp.transpose(pick[...]).astype(BF16)
        rest[...] = (
            x_ref[...].astype(F32) - jnp.dot(place[...], compact, preferred_element_type=F32)
        ).astype(BF16)
        for j in (1, 2, 3):
            count_copy(j - 1, counts.at[lax.rem(p + GROUP - j, GROUP)], peers[j - 1]).wait_recv()
        place_of = lax.broadcasted_iota(jnp.int32, (LIVE, HEAD), 0).astype(F32)
        for q in range(GROUP):
            flags[q * LIVE : (q + 1) * LIVE, :] = jnp.where(
                place_of < jnp.broadcast_to(counts[q, 0:1, :], (LIVE, HEAD)), 1.0, 0.0
            ).astype(BF16)

    def gate():
        pl.when(s == 1)(lambda: pl.semaphore_wait(turn, 1))

    def open_gate():
        @pl.when(s == 0)
        def _():
            pl.semaphore_signal(turn, inc=1, device_id={"section": 1 - s}, device_id_type=MESH)

    steps = {
        "a": ga.step, "c": gc.step, "z": line.step, "project": project, "attend": attend,
        "close": lambda c: copies.append(close(c)), "greet": greet, "prepare": prepare,
        "gate": gate, "open": open_gate,
    }
    for name, *at in ORDER:
        steps[name](*at)

    for j in (1, 2, 3):
        count_copy(j - 1, counts.at[p], peers[j - 1]).wait_send()
    ga.finish()
    gc.finish()
    line.finish()
    for copy in copies:
        copy.wait()


def body(acts, halting, norm_gain, qkv_weight, qk_gain, out_weight):
    vmem = pl.BlockSpec(memory_space=pltpu.VMEM)
    anywhere = pl.BlockSpec(memory_space=pl.ANY)
    out = pl.pallas_call(
        kernel,
        out_shape=jax.ShapeDtypeStruct((TOK, FEAT), BF16),
        in_specs=[vmem, vmem, vmem, vmem, anywhere, anywhere],
        out_specs=anywhere,
        scratch_shapes=[
            pltpu.VMEM((16 * FEAT, COLS), BF16),
            pltpu.VMEM((16 * WIDE, FEAT), BF16),
            pltpu.VMEM((SIDE, SIDE, LIVE, FEAT), BF16),
            pltpu.VMEM((ROWS, 16 * FEAT), BF16),
            pltpu.VMEM((ROWS, COLS), F32),
            pltpu.VMEM((GROUP, LIVE, 2 * WIDE), BF16),
            pltpu.VMEM((HEADS_HERE, LIVE, HEAD), BF16),
            pltpu.VMEM((GROUP, 8, 128), F32),
            pltpu.VMEM((GROUP * LIVE, HEAD), BF16),
            pltpu.VMEM((SIDE, SIDE, LIVE, WIDE), BF16),
            pltpu.VMEM((LIVE, TOK), F32),
            pltpu.VMEM((TOK, LIVE), BF16),
            pltpu.VMEM((TOK, FEAT), BF16),
            pltpu.VMEM((LIVE, FEAT), BF16),
            pltpu.VMEM((TOK, FEAT), BF16),
            pltpu.SemaphoreType.DMA((2,)),
            pltpu.SemaphoreType.DMA((len(PIECES_A) * 9,)),
            pltpu.SemaphoreType.DMA((len(PIECES_A) * 9,)),
            pltpu.SemaphoreType.DMA((len(PIECES_C) * 9,)),
            pltpu.SemaphoreType.DMA((len(PIECES_C) * 9,)),
            pltpu.SemaphoreType.DMA((len(PARTS) * 6,)),
            pltpu.SemaphoreType.DMA((len(PARTS) * 6,)),
            pltpu.SemaphoreType.DMA((3,)),
            pltpu.SemaphoreType.DMA((3,)),
            pltpu.SemaphoreType.DMA((CHUNKS,)),
            pltpu.SemaphoreType.DMA((CHUNKS,)),
            pltpu.SemaphoreType.REGULAR,
        ],
        compiler_params=pltpu.CompilerParams(
            collective_id=0, has_side_effects=True, vmem_limit_bytes=56 * 1024 * 1024
        ),
    )(acts[0], halting, norm_gain, qk_gain[0], qkv_weight[0], out_weight[0])
    return out[None]


def solution(mesh):
    return jax.shard_map(
        body,
        mesh=mesh,
        in_specs=(
            P("section", "dp", "mp"),
            P("section", "dp"),
            P("section", None),
            P("section", None, "mp"),
            P("section", None, "mp", None),
            P("section", None, "mp"),
        ),
        out_specs=P("section", "dp", "mp"),
        check_vma=False,
    )
```

```python
import functools
import math

import jax
import jax.numpy as jnp
from jax import lax
from jax.experimental import pallas as pl
from jax.experimental.pallas import tpu as pltpu
from jax.sharding import PartitionSpec as P

MESH = pl.DeviceIdType.MESH
HEAD = 128
GROUP = 4
SIDE = 4
TOK = 512
LIVE = 384
FEAT = 384
HEADS_HERE = 2
WIDE = HEADS_HERE * HEAD
COLS = 3 * WIDE
ROWS = 128
CHUNKS = LIVE // ROWS
SCALE = math.log2(math.e) / math.sqrt(HEAD)
F32 = jnp.float32
BF16 = jnp.bfloat16


PIECES_A = ((0, 32, 1, 0), (32, 32, 0, 0), (64, 64, 1, 0), (128, 64, 0, 0), (192, 64, 1, 0), (256, 64, 0, 0), (320, 32, 1, 0), (352, 32, 0, 0))
PIECES_C = ((0, 64, 1, 1), (64, 64, 0, 1), (128, 64, 1, 1), (192, 64, 0, 1), (256, 64, 1, 1), (320, 64, 0, 1))
PARTS = ((0, 64), (64, 128), (192, 128), (320, 64))

DIRECT = (3,)

ORDER = (
    ("a", 0, 0), ("a", 0, 1), ("a", 1, 0), ("a", 1, 1), ("gate",), ("a", 2, 0), ("a", 2, 1), ("a", 3, 0), ("a", 3, 1),
    ("greet",), ("a", 0, 2), ("a", 1, 2), ("a", 4, 0), ("a", 4, 1), ("a", 5, 0), ("a", 5, 1), ("a", 2, 2),
    ("a", 3, 2), ("a", 6, 0), ("a", 6, 1), ("a", 7, 0), ("a", 7, 1), ("a", 4, 2), ("a", 5, 2), ("prepare",),
    ("a", 0, 3), ("a", 1, 3), ("project", 0), ("z", 0, 0), ("ask", 0), ("a", 6, 2), ("a", 7, 2), ("open",), ("a", 2, 3),
    ("a", 3, 3), ("project", 1), ("z", 1, 0), ("ask", 1), ("z", 0, 1), ("a", 4, 3), ("a", 5, 3), ("project", 2), ("z", 2, 0), ("ask", 2),
    ("z", 1, 1), ("a", 6, 3), ("a", 7, 3), ("project", 3), ("z", 3, 0), ("ask", 3), ("z", 2, 1), ("z", 0, 2), ("z", 1, 2),
    ("z", 2, 2), ("z", 3, 2), ("attend", 0), ("c", 0, 0), ("c", 0, 1), ("c", 1, 0), ("c", 1, 1), ("attend", 1),
    ("c", 2, 0), ("c", 2, 1), ("c", 3, 0), ("c", 3, 1), ("attend", 2), ("c", 4, 0), ("c", 4, 1), ("c", 5, 0),
    ("c", 5, 1), ("c", 0, 2), ("c", 1, 2), ("c", 2, 2), ("c", 3, 2), ("c", 4, 2), ("c", 5, 2), ("c", 0, 3),
    ("c", 1, 3), ("c", 2, 3), ("c", 3, 3), ("c", 4, 3), ("c", 5, 3), ("c", 0, 4), ("c", 1, 4), ("close", 0),
    ("c", 2, 4), ("c", 3, 4), ("close", 1), ("c", 4, 4), ("c", 5, 4), ("close", 2),
)


class Gather:
    def __init__(self, buf, pieces, send, recv, x, y):
        self.buf, self.pieces, self.send, self.recv = buf, pieces, send, recv
        self.at = (y, x)
        self.started = []

    def device(self, axis, by):
        y, x = self.at
        if axis == 0:
            y = lax.rem(y + by + SIDE, SIDE)
        else:
            x = lax.rem(x + by + SIDE, SIDE)
        return {"mp": y * SIDE + x}

    def copy(self, n, k, src, dst, device):
        at = n * 9 + k
        return pltpu.make_async_remote_copy(
            src_ref=src,
            dst_ref=dst,
            send_sem=self.send.at[at],
            recv_sem=self.recv.at[at],
            device_id=device,
            device_id_type=MESH,
        )

    def plan(self, n):
        row, rows, first, way = self.pieces[n]
        whole = ((0, 1), (1, -1), (2, 2))
        sends = [[(k, (0, 1), 0, first, d) for k, d in whole]]
        if way == 0:
            sends += [[(3 + k, (0, 1), 0, 1 - first, d) for k, d in whole]]
            sends += [[(6 + k, (1, 3), 0, 1 - first, d) for k, d in whole]]
            waits = ((), (), (0,), (1, 2))
        else:
            sends += [[(3 + k, (0, 1), 0, 1 - first, d) for k, d in whole[:2]]]
            sends += [[(5 + k, (1, 3), 0, 1 - first, d) for k, d in whole[:2]]]
            sends += [[(7, (0, 2), -1, 1 - first, 1), (8, (2, 2), 1, 1 - first, -1)]]
            waits = ((), (), (0,), (1, 2), (3,))
        return sends, waits

    def ref(self, n, low, count, second):
        row, rows, first, _ = self.pieces[n]
        second = second % SIDE
        if count == 1:
            y, x = (second, low % SIDE) if first == 1 else (low % SIDE, second)
            return self.buf.at[y, x, pl.ds(row, rows), :]
        if first == 1:
            return self.buf.at[second, pl.ds(low, count), pl.ds(row, rows), :]
        return self.buf.at[pl.ds(low, count), second, pl.ds(row, rows), :]

    def ends(self, n, at, second, axis, by):
        low, count = at
        src = self.ref(n, low, count, second)
        if axis == self.pieces[n][2]:
            return src, self.ref(n, low - by, count, second)
        return src, self.ref(n, low, count, second - by)

    def step(self, n, stage):
        sends, waits = self.plan(n)
        for before in waits[stage]:
            for k, at, second, axis, by in sends[before]:
                _, dst = self.ends(n, at, second, axis, by)
                self.copy(n, k, dst, dst, self.device(axis, by)).wait_recv()
        if stage < len(sends):
            for k, at, second, axis, by in sends[stage]:
                copy = self.copy(n, k, *self.ends(n, at, second, axis, by), self.device(axis, by))
                copy.start()
                self.started.append(copy)

    def finish(self):
        for copy in self.started:
            copy.wait_send()


class Line:
    def __init__(self, kv, send, recv, z):
        self.kv, self.send, self.recv, self.z = kv, send, recv, z
        self.p = lax.rem(z, GROUP)
        self.started = []

    def copy(self, c, d, way, owner, device):
        at = (c * 3 + d - 1) * 2 + (0 if way > 0 else 1)
        ref = self.kv.at[owner, pl.ds(*PARTS[c])]
        return pltpu.make_async_remote_copy(
            src_ref=ref,
            dst_ref=ref,
            send_sem=self.send.at[at],
            recv_sem=self.recv.at[at],
            device_id={"dp": device},
            device_id_type=MESH,
        )

    def reaches(self, d, way):
        return self.p < GROUP - d if way > 0 else self.p >= d

    def comes(self, d, way):
        return self.p >= d if way > 0 else self.p < GROUP - d

    def passes(self, way):
        return self.p == (2 if way > 0 else 1)

    def own(self, c, d, way):
        return self.copy(c, d, way, self.p, self.z + way * d)

    def passed(self, c, way):
        return self.copy(c, 3, way, self.p - way * 2, self.z + way)

    def arrival(self, c, d, way):
        return self.copy(c, d, way, self.p - way * d, self.z - way)

    def far(self, c):
        return (1, 2, 3) if c in DIRECT else (1, 2)

    def step(self, c, stage):
        for d in (1, 2, 3):
            for way in (1, -1):
                if stage == 0 and d in self.far(c):
                    pl.when(self.reaches(d, way))(lambda: self.own(c, d, way).start())
                if stage == 1 and d == 3:

                    @pl.when(self.passes(way))
                    def _():
                        self.arrival(c, 2, way).wait_recv()
                        self.passed(c, way).start()

                if stage == 2:
                    here = self.comes(d, way)
                    if d == 2 and c not in DIRECT:
                        here = jnp.logical_and(here, jnp.logical_not(self.passes(way)))
                    pl.when(here)(lambda: self.arrival(c, d, way).wait_recv())
        if stage == 0:
            self.started.append(c)

    def finish(self):
        for c in self.started:
            for way in (1, -1):
                for d in self.far(c):
                    pl.when(self.reaches(d, way))(lambda: self.own(c, d, way).wait_send())
                if c not in DIRECT:
                    pl.when(self.passes(way))(lambda: self.passed(c, way).wait_send())


def normed(values, gain):
    mean = jnp.mean(values, axis=-1, keepdims=True)
    centred = values - mean
    spread = jnp.mean(centred * centred, axis=-1, keepdims=True)
    return centred * lax.rsqrt(spread + 1e-06) * gain


def kernel(
    x_ref, halt_ref, gain_ref, qk_ref, w_hbm, wo_hbm, out_ref,
    w, wo, xg, xn, kv, query, counts, flags, hg, pick, place, rest, result, outgoing,
    w_sem, a_send, a_recv, c_send, c_recv, z_send, z_recv, n_send, n_recv, o_send, o_recv, turn,
):
    z = lax.axis_index("dp")
    m = lax.axis_index("mp")
    s = lax.axis_index("section")
    x, y = lax.rem(m, SIDE), m // SIDE
    p = lax.rem(z, GROUP)
    base = z - p

    barrier = pltpu.get_barrier_semaphore()
    peers = [{"dp": base + lax.rem(p + j, GROUP)} for j in (1, 2, 3)]
    neighbours = [
        {"mp": y * SIDE + lax.rem(x + 1, SIDE)},
        {"mp": y * SIDE + lax.rem(x + SIDE - 1, SIDE)},
        {"mp": y * SIDE + lax.rem(x + 2, SIDE)},
        {"mp": lax.rem(y + 1, SIDE) * SIDE + x},
        {"mp": lax.rem(y + 2, SIDE) * SIDE + x},
        {"mp": lax.rem(y + SIDE - 1, SIDE) * SIDE + x},
        {"section": 1 - s},
    ]
    for device in neighbours + peers:
        pl.semaphore_signal(barrier, inc=1, device_id=device, device_id_type=MESH)

    load_w = pltpu.make_async_copy(w_hbm, w, w_sem.at[0])
    load_wo = pltpu.make_async_copy(wo_hbm, wo, w_sem.at[1])
    load_w.start()
    load_wo.start()

    live = jnp.where(halt_ref[...] > s, 1.0, 0.0)
    before = lax.broadcasted_iota(jnp.int32, (TOK, TOK), 0) < lax.broadcasted_iota(jnp.int32, (TOK, TOK), 1)
    rank = jnp.dot(
        jnp.broadcast_to(live, (16, TOK)).astype(BF16),
        jnp.where(before, 1.0, 0.0).astype(BF16),
        preferred_element_type=F32,
    )[0:1]
    count = jnp.sum(live, axis=-1, keepdims=True)
    rank = jnp.where(live > 0.5, rank, -1.0)
    row = lax.broadcasted_iota(jnp.int32, (LIVE, TOK), 0).astype(F32)
    chosen = jnp.broadcast_to(rank, (LIVE, TOK)) == jnp.minimum(row, jnp.broadcast_to(count, (LIVE, TOK)) - 1.0)
    first = jnp.where(chosen, 1.0, 0.0)
    pick[...] = jnp.where(row < jnp.broadcast_to(count, (LIVE, TOK)), first, 0.0)
    compact = jnp.dot(first.astype(BF16), x_ref[...], preferred_element_type=F32).astype(BF16)
    xg[0, 0] = compact
    counts[p] = jnp.broadcast_to(count, (8, 128))

    pl.semaphore_wait(barrier, 10)

    def from_here(b):
        return lax.rem(b // SIDE - y + SIDE, SIDE), lax.rem(b % SIDE - x + SIDE, SIDE)

    ga = Gather(xg, PIECES_A, a_send, a_recv, x, y)
    gc = Gather(hg, PIECES_C, c_send, c_recv, x, y)
    line = Line(kv, z_send, z_recv, z)

    def count_copy(j, ref, device):
        return pltpu.make_async_remote_copy(
            src_ref=ref,
            dst_ref=ref,
            send_sem=n_send.at[j],
            recv_sem=n_recv.at[j],
            device_id=device,
            device_id_type=MESH,
        )

    def project(c):
        low, rows = PARTS[c]
        for at in range(low, low + rows, 64):
            at = slice(at, at + 64)
            total = jnp.zeros((64, 1), F32)
            for b in range(16):
                total += jnp.sum(xg[*from_here(b), at].astype(F32), axis=-1, keepdims=True)
            mean = total * (1.0 / (16 * FEAT))
            square = jnp.zeros((64, 1), F32)
            for b in range(16):
                centred = xg[*from_here(b), at].astype(F32) - mean
                square += jnp.sum(centred * centred, axis=-1, keepdims=True)
            scale = lax.rsqrt(square * (1.0 / (16 * FEAT)) + 1e-06)
            for b in range(16):
                lanes = slice(b * FEAT, (b + 1) * FEAT)
                centred = xg[*from_here(b), at].astype(F32) - mean
                xn[at.start - low : at.stop - low, lanes] = (centred * scale * gain_ref[:, lanes]).astype(BF16)
        if c == 0:
            load_w.wait()
        real = lax.broadcasted_iota(jnp.int32, (rows, HEAD), 0).astype(F32) + low < jnp.broadcast_to(count, (rows, HEAD))
        at = slice(low, low + rows)
        for h in range(HEADS_HERE):
            col = h * 3 * HEAD + HEAD
            total = jnp.zeros((rows, 2 * HEAD), F32)
            for b in range(8):
                depth = slice(b * 2 * FEAT, (b + 1) * 2 * FEAT)
                total += jnp.dot(xn[:rows, depth], w[depth, col : col + 2 * HEAD], preferred_element_type=F32)
            kv[p, at, h * HEAD : (h + 1) * HEAD] = normed(total[:, :HEAD], qk_ref[1, h : h + 1, :]).astype(BF16)
            kv[p, at, WIDE + h * HEAD : WIDE + (h + 1) * HEAD] = jnp.where(real, total[:, HEAD:], 0.0).astype(BF16)

    def ask(c):
        low, rows = PARTS[c]
        total = jnp.zeros((rows, WIDE), F32)
        for b in range(8):
            depth = slice(b * 2 * FEAT, (b + 1) * 2 * FEAT)
            columns = jnp.concatenate([w[depth, :HEAD], w[depth, 3 * HEAD : 4 * HEAD]], axis=1)
            total += jnp.dot(xn[:rows, depth], columns, preferred_element_type=F32)
        for h in range(HEADS_HERE):
            query[h, low : low + rows] = normed(
                total[:, h * HEAD : (h + 1) * HEAD], qk_ref[0, h : h + 1, :]
            ).astype(BF16)

    def attend(c):
        for h in range(HEADS_HERE):
            keys = kv[:, :, h * HEAD : (h + 1) * HEAD].reshape(GROUP * LIVE, HEAD)
            values = kv[:, :, WIDE + h * HEAD : WIDE + (h + 1) * HEAD].reshape(GROUP * LIVE, HEAD)
            scores = (
                lax.dot_general(query[h, c * ROWS : (c + 1) * ROWS], keys, (((1,), (1,)), ((), ())), preferred_element_type=F32) * SCALE
            )
            top = jnp.max(scores, axis=-1, keepdims=True)
            weights = jnp.exp2(scores - top).astype(BF16)
            summed = jnp.dot(
                weights, jnp.concatenate([values, flags[...]], axis=1), preferred_element_type=F32
            )
            heads = (summed[:, :HEAD] / summed[:, HEAD:]).astype(BF16)
            hg[0, 0, c * ROWS : (c + 1) * ROWS, h * HEAD : (h + 1) * HEAD] = heads

    def close(c):
        if c == 0:
            load_wo.wait()
        total = jnp.zeros((ROWS, FEAT), F32)
        for b in range(SIDE):
            heads = jnp.concatenate(
                [hg[*from_here(b * SIDE + i), c * ROWS : (c + 1) * ROWS] for i in range(SIDE)], axis=1
            )
            total += jnp.dot(heads, wo[b * SIDE * WIDE : (b + 1) * SIDE * WIDE, :], preferred_element_type=F32)
        mine = xg[0, 0, c * ROWS : (c + 1) * ROWS].astype(F32)
        result[c * ROWS : (c + 1) * ROWS, :] = (mine + total).astype(BF16)
        low, high = c * ROWS, (c + 1) * ROWS if c < CHUNKS - 1 else TOK
        known = (c + 1) * ROWS
        placed = jnp.dot(place[low:high, :known], result[:known, :], preferred_element_type=F32)
        outgoing[low:high, :] = (rest[low:high, :].astype(F32) + placed).astype(BF16)
        copy = pltpu.make_async_remote_copy(
            src_ref=outgoing.at[pl.ds(low, high - low)],
            dst_ref=out_ref.at[pl.ds(low, high - low)],
            send_sem=o_send.at[c],
            recv_sem=o_recv.at[c],
            device_id={"section": 1 - s},
            device_id_type=MESH,
        )
        copy.start()
        return copy

    copies = []

    def greet():
        for j in (1, 2, 3):
            count_copy(j - 1, counts.at[p], peers[j - 1]).start()

    def prepare():
        place[...] = jnp.transpose(pick[...]).astype(BF16)
        rest[...] = (
            x_ref[...].astype(F32) - jnp.dot(place[...], compact, preferred_element_type=F32)
        ).astype(BF16)
        for j in (1, 2, 3):
            count_copy(j - 1, counts.at[lax.rem(p + GROUP - j, GROUP)], peers[j - 1]).wait_recv()
        place_of = lax.broadcasted_iota(jnp.int32, (LIVE, HEAD), 0).astype(F32)
        for q in range(GROUP):
            flags[q * LIVE : (q + 1) * LIVE, :] = jnp.where(
                place_of < jnp.broadcast_to(counts[q, 0:1, :], (LIVE, HEAD)), 1.0, 0.0
            ).astype(BF16)

    def gate():
        pl.when(s == 1)(lambda: pl.semaphore_wait(turn, 1))

    def open_gate():
        @pl.when(s == 0)
        def _():
            pl.semaphore_signal(turn, inc=1, device_id={"section": 1 - s}, device_id_type=MESH)

    steps = {
        "a": ga.step, "c": gc.step, "z": line.step, "project": project, "ask": ask, "attend": attend,
        "close": lambda c: copies.append(close(c)), "greet": greet, "prepare": prepare,
        "gate": gate, "open": open_gate,
    }
    for name, *at in ORDER:
        steps[name](*at)

    for j in (1, 2, 3):
        count_copy(j - 1, counts.at[p], peers[j - 1]).wait_send()
    ga.finish()
    gc.finish()
    line.finish()
    for copy in copies:
        copy.wait()


def body(acts, halting, norm_gain, qkv_weight, qk_gain, out_weight):
    vmem = pl.BlockSpec(memory_space=pltpu.VMEM)
    anywhere = pl.BlockSpec(memory_space=pl.ANY)
    out = pl.pallas_call(
        kernel,
        out_shape=jax.ShapeDtypeStruct((TOK, FEAT), BF16),
        in_specs=[vmem, vmem, vmem, vmem, anywhere, anywhere],
        out_specs=anywhere,
        scratch_shapes=[
            pltpu.VMEM((16 * FEAT, COLS), BF16),
            pltpu.VMEM((16 * WIDE, FEAT), BF16),
            pltpu.VMEM((SIDE, SIDE, LIVE, FEAT), BF16),
            pltpu.VMEM((ROWS, 16 * FEAT), BF16),
            pltpu.VMEM((GROUP, LIVE, 2 * WIDE), BF16),
            pltpu.VMEM((HEADS_HERE, LIVE, HEAD), BF16),
            pltpu.VMEM((GROUP, 8, 128), F32),
            pltpu.VMEM((GROUP * LIVE, HEAD), BF16),
            pltpu.VMEM((SIDE, SIDE, LIVE, WIDE), BF16),
            pltpu.VMEM((LIVE, TOK), F32),
            pltpu.VMEM((TOK, LIVE), BF16),
            pltpu.VMEM((TOK, FEAT), BF16),
            pltpu.VMEM((LIVE, FEAT), BF16),
            pltpu.VMEM((TOK, FEAT), BF16),
            pltpu.SemaphoreType.DMA((2,)),
            pltpu.SemaphoreType.DMA((len(PIECES_A) * 9,)),
            pltpu.SemaphoreType.DMA((len(PIECES_A) * 9,)),
            pltpu.SemaphoreType.DMA((len(PIECES_C) * 9,)),
            pltpu.SemaphoreType.DMA((len(PIECES_C) * 9,)),
            pltpu.SemaphoreType.DMA((len(PARTS) * 6,)),
            pltpu.SemaphoreType.DMA((len(PARTS) * 6,)),
            pltpu.SemaphoreType.DMA((3,)),
            pltpu.SemaphoreType.DMA((3,)),
            pltpu.SemaphoreType.DMA((CHUNKS,)),
            pltpu.SemaphoreType.DMA((CHUNKS,)),
            pltpu.SemaphoreType.REGULAR,
        ],
        compiler_params=pltpu.CompilerParams(
            collective_id=0, has_side_effects=True, vmem_limit_bytes=56 * 1024 * 1024
        ),
    )(acts[0], halting, norm_gain, qk_gain[0], qkv_weight[0], out_weight[0])
    return out[None]


def solution(mesh):
    return jax.shard_map(
        body,
        mesh=mesh,
        in_specs=(
            P("section", "dp", "mp"),
            P("section", "dp"),
            P("section", None),
            P("section", None, "mp"),
            P("section", None, "mp", None),
            P("section", None, "mp"),
        ),
        out_specs=P("section", "dp", "mp"),
        check_vma=False,
    )
```

```python
import functools
import math

import jax
import jax.numpy as jnp
from jax import lax
from jax.experimental import pallas as pl
from jax.experimental.pallas import tpu as pltpu
from jax.sharding import PartitionSpec as P

MESH = pl.DeviceIdType.MESH
HEAD = 128
GROUP = 4
SIDE = 4
TOK = 512
LIVE = 384
FEAT = 384
HEADS_HERE = 2
WIDE = HEADS_HERE * HEAD
COLS = 3 * WIDE
ROWS = 128
CHUNKS = LIVE // ROWS
SCALE = math.log2(math.e) / math.sqrt(HEAD)
F32 = jnp.float32
BF16 = jnp.bfloat16


PIECES_A = ((0, 32, 1, 0), (32, 32, 0, 0), (64, 64, 1, 0), (128, 64, 0, 0), (192, 64, 1, 0), (256, 64, 0, 0), (320, 32, 1, 0), (352, 32, 0, 0))
PIECES_C = ((0, 64, 1, 1), (64, 64, 0, 1), (128, 64, 1, 1), (192, 64, 0, 1), (256, 64, 1, 1), (320, 64, 0, 1))
PARTS = ((0, 64), (64, 128), (192, 128), (320, 64))

DIRECT = (3,)

ORDER = (
    ("a", 0, 0), ("a", 0, 1), ("a", 1, 0), ("a", 1, 1), ("gate",), ("a", 2, 0), ("a", 2, 1), ("a", 3, 0), ("a", 3, 1),
    ("greet",), ("a", 0, 2), ("a", 1, 2), ("a", 4, 0), ("a", 4, 1), ("a", 5, 0), ("a", 5, 1), ("a", 2, 2),
    ("a", 3, 2), ("a", 6, 0), ("a", 6, 1), ("a", 7, 0), ("a", 7, 1), ("a", 4, 2), ("a", 5, 2), ("prepare",),
    ("a", 0, 3), ("a", 1, 3), ("project", 0), ("z", 0, 0), ("ask", 0), ("a", 6, 2), ("a", 7, 2), ("open",), ("a", 2, 3),
    ("a", 3, 3), ("project", 1), ("z", 1, 0), ("z", 0, 1), ("ask", 1), ("a", 4, 3), ("a", 5, 3), ("project", 2), ("z", 2, 0), ("z", 1, 1),
    ("ask", 2), ("a", 6, 3), ("a", 7, 3), ("project", 3), ("z", 3, 0), ("z", 2, 1), ("ask", 3), ("z", 0, 2), ("z", 1, 2),
    ("z", 2, 2), ("z", 3, 2), ("attend", 0), ("c", 0, 0), ("c", 0, 1), ("c", 1, 0), ("c", 1, 1), ("attend", 1),
    ("c", 2, 0), ("c", 2, 1), ("c", 3, 0), ("c", 3, 1), ("attend", 2), ("c", 4, 0), ("c", 4, 1), ("c", 5, 0),
    ("c", 5, 1), ("c", 0, 2), ("c", 1, 2), ("c", 2, 2), ("c", 3, 2), ("c", 4, 2), ("c", 5, 2), ("c", 0, 3),
    ("c", 1, 3), ("c", 2, 3), ("c", 3, 3), ("c", 4, 3), ("c", 5, 3), ("c", 0, 4), ("c", 1, 4), ("close", 0),
    ("c", 2, 4), ("c", 3, 4), ("close", 1), ("c", 4, 4), ("c", 5, 4), ("close", 2),
)


class Gather:
    def __init__(self, buf, pieces, send, recv, x, y):
        self.buf, self.pieces, self.send, self.recv = buf, pieces, send, recv
        self.at = (y, x)
        self.started = []

    def device(self, axis, by):
        y, x = self.at
        if axis == 0:
            y = lax.rem(y + by + SIDE, SIDE)
        else:
            x = lax.rem(x + by + SIDE, SIDE)
        return {"mp": y * SIDE + x}

    def copy(self, n, k, src, dst, device):
        at = n * 9 + k
        return pltpu.make_async_remote_copy(
            src_ref=src,
            dst_ref=dst,
            send_sem=self.send.at[at],
            recv_sem=self.recv.at[at],
            device_id=device,
            device_id_type=MESH,
        )

    def plan(self, n):
        row, rows, first, way = self.pieces[n]
        whole = ((0, 1), (1, -1), (2, 2))
        sends = [[(k, (0, 1), 0, first, d) for k, d in whole]]
        if way == 0:
            sends += [[(3 + k, (0, 1), 0, 1 - first, d) for k, d in whole]]
            sends += [[(6 + k, (1, 3), 0, 1 - first, d) for k, d in whole]]
            waits = ((), (), (0,), (1, 2))
        else:
            sends += [[(3 + k, (0, 1), 0, 1 - first, d) for k, d in whole[:2]]]
            sends += [[(5 + k, (1, 3), 0, 1 - first, d) for k, d in whole[:2]]]
            sends += [[(7, (0, 2), -1, 1 - first, 1), (8, (2, 2), 1, 1 - first, -1)]]
            waits = ((), (), (0,), (1, 2), (3,))
        return sends, waits

    def ref(self, n, low, count, second):
        row, rows, first, _ = self.pieces[n]
        second = second % SIDE
        if count == 1:
            y, x = (second, low % SIDE) if first == 1 else (low % SIDE, second)
            return self.buf.at[y, x, pl.ds(row, rows), :]
        if first == 1:
            return self.buf.at[second, pl.ds(low, count), pl.ds(row, rows), :]
        return self.buf.at[pl.ds(low, count), second, pl.ds(row, rows), :]

    def ends(self, n, at, second, axis, by):
        low, count = at
        src = self.ref(n, low, count, second)
        if axis == self.pieces[n][2]:
            return src, self.ref(n, low - by, count, second)
        return src, self.ref(n, low, count, second - by)

    def step(self, n, stage):
        sends, waits = self.plan(n)
        for before in waits[stage]:
            for k, at, second, axis, by in sends[before]:
                _, dst = self.ends(n, at, second, axis, by)
                self.copy(n, k, dst, dst, self.device(axis, by)).wait_recv()
        if stage < len(sends):
            for k, at, second, axis, by in sends[stage]:
                copy = self.copy(n, k, *self.ends(n, at, second, axis, by), self.device(axis, by))
                copy.start()
                self.started.append(copy)

    def finish(self):
        for copy in self.started:
            copy.wait_send()


class Line:
    def __init__(self, kv, send, recv, z):
        self.kv, self.send, self.recv, self.z = kv, send, recv, z
        self.p = lax.rem(z, GROUP)
        self.started = []

    def copy(self, c, d, way, owner, device):
        at = (c * 3 + d - 1) * 2 + (0 if way > 0 else 1)
        ref = self.kv.at[owner, pl.ds(*PARTS[c])]
        return pltpu.make_async_remote_copy(
            src_ref=ref,
            dst_ref=ref,
            send_sem=self.send.at[at],
            recv_sem=self.recv.at[at],
            device_id={"dp": device},
            device_id_type=MESH,
        )

    def reaches(self, d, way):
        return self.p < GROUP - d if way > 0 else self.p >= d

    def comes(self, d, way):
        return self.p >= d if way > 0 else self.p < GROUP - d

    def passes(self, way):
        return self.p == (2 if way > 0 else 1)

    def own(self, c, d, way):
        return self.copy(c, d, way, self.p, self.z + way * d)

    def passed(self, c, way):
        return self.copy(c, 3, way, self.p - way * 2, self.z + way)

    def arrival(self, c, d, way):
        return self.copy(c, d, way, self.p - way * d, self.z - way)

    def far(self, c):
        return (1, 2, 3) if c in DIRECT else (1, 2)

    def step(self, c, stage):
        for d in (1, 2, 3):
            for way in (1, -1):
                if stage == 0 and d in self.far(c):
                    pl.when(self.reaches(d, way))(lambda: self.own(c, d, way).start())
                if stage == 1 and d == 3:

                    @pl.when(self.passes(way))
                    def _():
                        self.arrival(c, 2, way).wait_recv()
                        self.passed(c, way).start()

                if stage == 2:
                    here = self.comes(d, way)
                    if d == 2 and c not in DIRECT:
                        here = jnp.logical_and(here, jnp.logical_not(self.passes(way)))
                    pl.when(here)(lambda: self.arrival(c, d, way).wait_recv())
        if stage == 0:
            self.started.append(c)

    def finish(self):
        for c in self.started:
            for way in (1, -1):
                for d in self.far(c):
                    pl.when(self.reaches(d, way))(lambda: self.own(c, d, way).wait_send())
                if c not in DIRECT:
                    pl.when(self.passes(way))(lambda: self.passed(c, way).wait_send())


def normed(values, gain):
    mean = jnp.mean(values, axis=-1, keepdims=True)
    centred = values - mean
    spread = jnp.mean(centred * centred, axis=-1, keepdims=True)
    return centred * lax.rsqrt(spread + 1e-06) * gain


def kernel(
    x_ref, halt_ref, gain_ref, qk_ref, w_hbm, wo_hbm, out_ref,
    w, wo, xg, xn, kv, query, counts, flags, hg, pick, place, rest, result, outgoing,
    w_sem, a_send, a_recv, c_send, c_recv, z_send, z_recv, n_send, n_recv, o_send, o_recv, turn,
):
    z = lax.axis_index("dp")
    m = lax.axis_index("mp")
    s = lax.axis_index("section")
    x, y = lax.rem(m, SIDE), m // SIDE
    p = lax.rem(z, GROUP)
    base = z - p

    barrier = pltpu.get_barrier_semaphore()
    peers = [{"dp": base + lax.rem(p + j, GROUP)} for j in (1, 2, 3)]
    neighbours = [
        {"mp": y * SIDE + lax.rem(x + 1, SIDE)},
        {"mp": y * SIDE + lax.rem(x + SIDE - 1, SIDE)},
        {"mp": y * SIDE + lax.rem(x + 2, SIDE)},
        {"mp": lax.rem(y + 1, SIDE) * SIDE + x},
        {"mp": lax.rem(y + 2, SIDE) * SIDE + x},
        {"mp": lax.rem(y + SIDE - 1, SIDE) * SIDE + x},
        {"section": 1 - s},
    ]
    for device in neighbours + peers:
        pl.semaphore_signal(barrier, inc=1, device_id=device, device_id_type=MESH)

    load_w = pltpu.make_async_copy(w_hbm, w, w_sem.at[0])
    load_wo = pltpu.make_async_copy(wo_hbm, wo, w_sem.at[1])
    load_w.start()
    load_wo.start()

    live = jnp.where(halt_ref[...] > s, 1.0, 0.0)
    before = lax.broadcasted_iota(jnp.int32, (TOK, TOK), 0) < lax.broadcasted_iota(jnp.int32, (TOK, TOK), 1)
    rank = jnp.dot(
        jnp.broadcast_to(live, (16, TOK)).astype(BF16),
        jnp.where(before, 1.0, 0.0).astype(BF16),
        preferred_element_type=F32,
    )[0:1]
    count = jnp.sum(live, axis=-1, keepdims=True)
    rank = jnp.where(live > 0.5, rank, -1.0)
    row = lax.broadcasted_iota(jnp.int32, (LIVE, TOK), 0).astype(F32)
    chosen = jnp.broadcast_to(rank, (LIVE, TOK)) == jnp.minimum(row, jnp.broadcast_to(count, (LIVE, TOK)) - 1.0)
    first = jnp.where(chosen, 1.0, 0.0)
    pick[...] = jnp.where(row < jnp.broadcast_to(count, (LIVE, TOK)), first, 0.0)
    compact = jnp.dot(first.astype(BF16), x_ref[...], preferred_element_type=F32).astype(BF16)
    xg[0, 0] = compact
    counts[p] = jnp.broadcast_to(count, (8, 128))

    pl.semaphore_wait(barrier, 10)

    def from_here(b):
        return lax.rem(b // SIDE - y + SIDE, SIDE), lax.rem(b % SIDE - x + SIDE, SIDE)

    ga = Gather(xg, PIECES_A, a_send, a_recv, x, y)
    gc = Gather(hg, PIECES_C, c_send, c_recv, x, y)
    line = Line(kv, z_send, z_recv, z)

    def count_copy(j, ref, device):
        return pltpu.make_async_remote_copy(
            src_ref=ref,
            dst_ref=ref,
            send_sem=n_send.at[j],
            recv_sem=n_recv.at[j],
            device_id=device,
            device_id_type=MESH,
        )

    def project(c):
        low, rows = PARTS[c]
        for at in range(low, low + rows, 64):
            at = slice(at, at + 64)
            total = jnp.zeros((64, 1), F32)
            for b in range(16):
                total += jnp.sum(xg[*from_here(b), at].astype(F32), axis=-1, keepdims=True)
            mean = total * (1.0 / (16 * FEAT))
            square = jnp.zeros((64, 1), F32)
            for b in range(16):
                centred = xg[*from_here(b), at].astype(F32) - mean
                square += jnp.sum(centred * centred, axis=-1, keepdims=True)
            scale = lax.rsqrt(square * (1.0 / (16 * FEAT)) + 1e-06)
            for b in range(16):
                lanes = slice(b * FEAT, (b + 1) * FEAT)
                centred = xg[*from_here(b), at].astype(F32) - mean
                xn[at.start - low : at.stop - low, lanes] = (centred * scale * gain_ref[:, lanes]).astype(BF16)
        if c == 0:
            load_w.wait()
        real = lax.broadcasted_iota(jnp.int32, (rows, HEAD), 0).astype(F32) + low < jnp.broadcast_to(count, (rows, HEAD))
        at = slice(low, low + rows)
        for h in range(HEADS_HERE):
            col = h * 3 * HEAD + HEAD
            total = jnp.zeros((rows, 2 * HEAD), F32)
            for b in range(8):
                depth = slice(b * 2 * FEAT, (b + 1) * 2 * FEAT)
                total += jnp.dot(xn[:rows, depth], w[depth, col : col + 2 * HEAD], preferred_element_type=F32)
            kv[p, at, h * HEAD : (h + 1) * HEAD] = normed(total[:, :HEAD], qk_ref[1, h : h + 1, :]).astype(BF16)
            kv[p, at, WIDE + h * HEAD : WIDE + (h + 1) * HEAD] = jnp.where(real, total[:, HEAD:], 0.0).astype(BF16)

    def ask(c):
        low, rows = PARTS[c]
        total = jnp.zeros((rows, WIDE), F32)
        for b in range(8):
            depth = slice(b * 2 * FEAT, (b + 1) * 2 * FEAT)
            columns = jnp.concatenate([w[depth, :HEAD], w[depth, 3 * HEAD : 4 * HEAD]], axis=1)
            total += jnp.dot(xn[:rows, depth], columns, preferred_element_type=F32)
        for h in range(HEADS_HERE):
            query[h, low : low + rows] = normed(
                total[:, h * HEAD : (h + 1) * HEAD], qk_ref[0, h : h + 1, :]
            ).astype(BF16)

    def attend(c):
        for h in range(HEADS_HERE):
            keys = kv[:, :, h * HEAD : (h + 1) * HEAD].reshape(GROUP * LIVE, HEAD)
            values = kv[:, :, WIDE + h * HEAD : WIDE + (h + 1) * HEAD].reshape(GROUP * LIVE, HEAD)
            scores = (
                lax.dot_general(query[h, c * ROWS : (c + 1) * ROWS], keys, (((1,), (1,)), ((), ())), preferred_element_type=F32) * SCALE
            )
            top = jnp.max(scores, axis=-1, keepdims=True)
            weights = jnp.exp2(scores - top).astype(BF16)
            summed = jnp.dot(
                weights, jnp.concatenate([values, flags[...]], axis=1), preferred_element_type=F32
            )
            heads = (summed[:, :HEAD] / summed[:, HEAD:]).astype(BF16)
            hg[0, 0, c * ROWS : (c + 1) * ROWS, h * HEAD : (h + 1) * HEAD] = heads

    def close(c):
        if c == 0:
            load_wo.wait()
        total = jnp.zeros((ROWS, FEAT), F32)
        for b in range(SIDE):
            heads = jnp.concatenate(
                [hg[*from_here(b * SIDE + i), c * ROWS : (c + 1) * ROWS] for i in range(SIDE)], axis=1
            )
            total += jnp.dot(heads, wo[b * SIDE * WIDE : (b + 1) * SIDE * WIDE, :], preferred_element_type=F32)
        mine = xg[0, 0, c * ROWS : (c + 1) * ROWS].astype(F32)
        result[c * ROWS : (c + 1) * ROWS, :] = (mine + total).astype(BF16)
        low, high = c * ROWS, (c + 1) * ROWS if c < CHUNKS - 1 else TOK
        known = (c + 1) * ROWS
        placed = jnp.dot(place[low:high, :known], result[:known, :], preferred_element_type=F32)
        outgoing[low:high, :] = (rest[low:high, :].astype(F32) + placed).astype(BF16)
        copy = pltpu.make_async_remote_copy(
            src_ref=outgoing.at[pl.ds(low, high - low)],
            dst_ref=out_ref.at[pl.ds(low, high - low)],
            send_sem=o_send.at[c],
            recv_sem=o_recv.at[c],
            device_id={"section": 1 - s},
            device_id_type=MESH,
        )
        copy.start()
        return copy

    copies = []

    def greet():
        for j in (1, 2, 3):
            count_copy(j - 1, counts.at[p], peers[j - 1]).start()

    def prepare():
        place[...] = jnp.transpose(pick[...]).astype(BF16)
        rest[...] = (
            x_ref[...].astype(F32) - jnp.dot(place[...], compact, preferred_element_type=F32)
        ).astype(BF16)
        for j in (1, 2, 3):
            count_copy(j - 1, counts.at[lax.rem(p + GROUP - j, GROUP)], peers[j - 1]).wait_recv()
        place_of = lax.broadcasted_iota(jnp.int32, (LIVE, HEAD), 0).astype(F32)
        for q in range(GROUP):
            flags[q * LIVE : (q + 1) * LIVE, :] = jnp.where(
                place_of < jnp.broadcast_to(counts[q, 0:1, :], (LIVE, HEAD)), 1.0, 0.0
            ).astype(BF16)

    def gate():
        pl.when(s == 1)(lambda: pl.semaphore_wait(turn, 1))

    def open_gate():
        @pl.when(s == 0)
        def _():
            pl.semaphore_signal(turn, inc=1, device_id={"section": 1 - s}, device_id_type=MESH)

    steps = {
        "a": ga.step, "c": gc.step, "z": line.step, "project": project, "ask": ask, "attend": attend,
        "close": lambda c: copies.append(close(c)), "greet": greet, "prepare": prepare,
        "gate": gate, "open": open_gate,
    }
    for name, *at in ORDER:
        steps[name](*at)

    for j in (1, 2, 3):
        count_copy(j - 1, counts.at[p], peers[j - 1]).wait_send()
    ga.finish()
    gc.finish()
    line.finish()
    for copy in copies:
        copy.wait()


def body(acts, halting, norm_gain, qkv_weight, qk_gain, out_weight):
    vmem = pl.BlockSpec(memory_space=pltpu.VMEM)
    anywhere = pl.BlockSpec(memory_space=pl.ANY)
    out = pl.pallas_call(
        kernel,
        out_shape=jax.ShapeDtypeStruct((TOK, FEAT), BF16),
        in_specs=[vmem, vmem, vmem, vmem, anywhere, anywhere],
        out_specs=anywhere,
        scratch_shapes=[
            pltpu.VMEM((16 * FEAT, COLS), BF16),
            pltpu.VMEM((16 * WIDE, FEAT), BF16),
            pltpu.VMEM((SIDE, SIDE, LIVE, FEAT), BF16),
            pltpu.VMEM((ROWS, 16 * FEAT), BF16),
            pltpu.VMEM((GROUP, LIVE, 2 * WIDE), BF16),
            pltpu.VMEM((HEADS_HERE, LIVE, HEAD), BF16),
            pltpu.VMEM((GROUP, 8, 128), F32),
            pltpu.VMEM((GROUP * LIVE, HEAD), BF16),
            pltpu.VMEM((SIDE, SIDE, LIVE, WIDE), BF16),
            pltpu.VMEM((LIVE, TOK), F32),
            pltpu.VMEM((TOK, LIVE), BF16),
            pltpu.VMEM((TOK, FEAT), BF16),
            pltpu.VMEM((LIVE, FEAT), BF16),
            pltpu.VMEM((TOK, FEAT), BF16),
            pltpu.SemaphoreType.DMA((2,)),
            pltpu.SemaphoreType.DMA((len(PIECES_A) * 9,)),
            pltpu.SemaphoreType.DMA((len(PIECES_A) * 9,)),
            pltpu.SemaphoreType.DMA((len(PIECES_C) * 9,)),
            pltpu.SemaphoreType.DMA((len(PIECES_C) * 9,)),
            pltpu.SemaphoreType.DMA((len(PARTS) * 6,)),
            pltpu.SemaphoreType.DMA((len(PARTS) * 6,)),
            pltpu.SemaphoreType.DMA((3,)),
            pltpu.SemaphoreType.DMA((3,)),
            pltpu.SemaphoreType.DMA((CHUNKS,)),
            pltpu.SemaphoreType.DMA((CHUNKS,)),
            pltpu.SemaphoreType.REGULAR,
        ],
        compiler_params=pltpu.CompilerParams(
            collective_id=0, has_side_effects=True, vmem_limit_bytes=56 * 1024 * 1024
        ),
    )(acts[0], halting, norm_gain, qk_gain[0], qkv_weight[0], out_weight[0])
    return out[None]


def solution(mesh):
    return jax.shard_map(
        body,
        mesh=mesh,
        in_specs=(
            P("section", "dp", "mp"),
            P("section", "dp"),
            P("section", None),
            P("section", None, "mp"),
            P("section", None, "mp", None),
            P("section", None, "mp"),
        ),
        out_specs=P("section", "dp", "mp"),
        check_vma=False,
    )
```

```python
import functools
import math

import jax
import jax.numpy as jnp
from jax import lax
from jax.experimental import pallas as pl
from jax.experimental.pallas import tpu as pltpu
from jax.sharding import PartitionSpec as P

MESH = pl.DeviceIdType.MESH
HEAD = 128
GROUP = 4
SIDE = 4
TOK = 512
LIVE = 384
FEAT = 384
HEADS_HERE = 2
WIDE = HEADS_HERE * HEAD
COLS = 3 * WIDE
ROWS = 128
CHUNKS = LIVE // ROWS
SCALE = math.log2(math.e) / math.sqrt(HEAD)
F32 = jnp.float32
BF16 = jnp.bfloat16


PIECES_A = ((0, 32, 1, 0), (32, 32, 0, 0), (64, 64, 1, 0), (128, 64, 0, 0), (192, 64, 1, 0), (256, 64, 0, 0), (320, 32, 1, 0), (352, 32, 0, 0))
PIECES_C = ((0, 64, 1, 1), (64, 64, 0, 1), (128, 64, 1, 1), (192, 64, 0, 1), (256, 64, 1, 0), (320, 64, 0, 0))
PARTS = ((0, 64), (64, 128), (192, 128), (320, 64))

DIRECT = (3,)

ORDER = (
    ("a", 0, 0), ("a", 0, 1), ("a", 1, 0), ("a", 1, 1), ("gate",), ("a", 2, 0), ("a", 2, 1), ("a", 3, 0), ("a", 3, 1),
    ("greet",), ("a", 0, 2), ("a", 1, 2), ("a", 4, 0), ("a", 4, 1), ("a", 5, 0), ("a", 5, 1), ("a", 2, 2),
    ("a", 3, 2), ("a", 6, 0), ("a", 6, 1), ("a", 7, 0), ("a", 7, 1), ("a", 4, 2), ("a", 5, 2), ("prepare",),
    ("a", 0, 3), ("a", 1, 3), ("project", 0), ("z", 0, 0), ("ask", 0), ("a", 6, 2), ("a", 7, 2), ("open",), ("a", 2, 3),
    ("a", 3, 3), ("project", 1), ("z", 1, 0), ("ask", 1), ("z", 0, 1), ("a", 4, 3), ("a", 5, 3), ("project", 2), ("z", 2, 0), ("ask", 2),
    ("z", 1, 1), ("a", 6, 3), ("a", 7, 3), ("project", 3), ("z", 3, 0), ("ask", 3), ("z", 2, 1), ("z", 0, 2), ("z", 1, 2),
    ("z", 2, 2), ("z", 3, 2), ("attend", 0), ("c", 0, 0), ("c", 0, 1), ("c", 1, 0), ("c", 1, 1), ("attend", 1),
    ("c", 2, 0), ("c", 2, 1), ("c", 3, 0), ("c", 3, 1), ("attend", 2), ("c", 4, 0), ("c", 4, 1), ("c", 5, 0),
    ("c", 5, 1), ("c", 0, 2), ("c", 1, 2), ("c", 2, 2), ("c", 3, 2), ("c", 4, 2), ("c", 5, 2), ("c", 0, 3),
    ("c", 1, 3), ("c", 2, 3), ("c", 3, 3), ("c", 0, 4), ("c", 1, 4), ("close", 0),
    ("c", 2, 4), ("c", 3, 4), ("close", 1), ("c", 4, 3), ("c", 5, 3), ("close", 2),
)


class Gather:
    def __init__(self, buf, pieces, send, recv, x, y):
        self.buf, self.pieces, self.send, self.recv = buf, pieces, send, recv
        self.at = (y, x)
        self.started = []

    def device(self, axis, by):
        y, x = self.at
        if axis == 0:
            y = lax.rem(y + by + SIDE, SIDE)
        else:
            x = lax.rem(x + by + SIDE, SIDE)
        return {"mp": y * SIDE + x}

    def copy(self, n, k, src, dst, device):
        at = n * 9 + k
        return pltpu.make_async_remote_copy(
            src_ref=src,
            dst_ref=dst,
            send_sem=self.send.at[at],
            recv_sem=self.recv.at[at],
            device_id=device,
            device_id_type=MESH,
        )

    def plan(self, n):
        row, rows, first, way = self.pieces[n]
        whole = ((0, 1), (1, -1), (2, 2))
        sends = [[(k, (0, 1), 0, first, d) for k, d in whole]]
        if way == 0:
            sends += [[(3 + k, (0, 1), 0, 1 - first, d) for k, d in whole]]
            sends += [[(6 + k, (1, 3), 0, 1 - first, d) for k, d in whole]]
            waits = ((), (), (0,), (1, 2))
        else:
            sends += [[(3 + k, (0, 1), 0, 1 - first, d) for k, d in whole[:2]]]
            sends += [[(5 + k, (1, 3), 0, 1 - first, d) for k, d in whole[:2]]]
            sends += [[(7, (0, 2), -1, 1 - first, 1), (8, (2, 2), 1, 1 - first, -1)]]
            waits = ((), (), (0,), (1, 2), (3,))
        return sends, waits

    def ref(self, n, low, count, second):
        row, rows, first, _ = self.pieces[n]
        second = second % SIDE
        if count == 1:
            y, x = (second, low % SIDE) if first == 1 else (low % SIDE, second)
            return self.buf.at[y, x, pl.ds(row, rows), :]
        if first == 1:
            return self.buf.at[second, pl.ds(low, count), pl.ds(row, rows), :]
        return self.buf.at[pl.ds(low, count), second, pl.ds(row, rows), :]

    def ends(self, n, at, second, axis, by):
        low, count = at
        src = self.ref(n, low, count, second)
        if axis == self.pieces[n][2]:
            return src, self.ref(n, low - by, count, second)
        return src, self.ref(n, low, count, second - by)

    def step(self, n, stage):
        sends, waits = self.plan(n)
        for before in waits[stage]:
            for k, at, second, axis, by in sends[before]:
                _, dst = self.ends(n, at, second, axis, by)
                self.copy(n, k, dst, dst, self.device(axis, by)).wait_recv()
        if stage < len(sends):
            for k, at, second, axis, by in sends[stage]:
                copy = self.copy(n, k, *self.ends(n, at, second, axis, by), self.device(axis, by))
                copy.start()
                self.started.append(copy)

    def finish(self):
        for copy in self.started:
            copy.wait_send()


class Line:
    def __init__(self, kv, send, recv, z):
        self.kv, self.send, self.recv, self.z = kv, send, recv, z
        self.p = lax.rem(z, GROUP)
        self.started = []

    def copy(self, c, d, way, owner, device):
        at = (c * 3 + d - 1) * 2 + (0 if way > 0 else 1)
        ref = self.kv.at[owner, pl.ds(*PARTS[c])]
        return pltpu.make_async_remote_copy(
            src_ref=ref,
            dst_ref=ref,
            send_sem=self.send.at[at],
            recv_sem=self.recv.at[at],
            device_id={"dp": device},
            device_id_type=MESH,
        )

    def reaches(self, d, way):
        return self.p < GROUP - d if way > 0 else self.p >= d

    def comes(self, d, way):
        return self.p >= d if way > 0 else self.p < GROUP - d

    def passes(self, way):
        return self.p == (2 if way > 0 else 1)

    def own(self, c, d, way):
        return self.copy(c, d, way, self.p, self.z + way * d)

    def passed(self, c, way):
        return self.copy(c, 3, way, self.p - way * 2, self.z + way)

    def arrival(self, c, d, way):
        return self.copy(c, d, way, self.p - way * d, self.z - way)

    def far(self, c):
        return (1, 2, 3) if c in DIRECT else (1, 2)

    def step(self, c, stage):
        for d in (1, 2, 3):
            for way in (1, -1):
                if stage == 0 and d in self.far(c):
                    pl.when(self.reaches(d, way))(lambda: self.own(c, d, way).start())
                if stage == 1 and d == 3:

                    @pl.when(self.passes(way))
                    def _():
                        self.arrival(c, 2, way).wait_recv()
                        self.passed(c, way).start()

                if stage == 2:
                    here = self.comes(d, way)
                    if d == 2 and c not in DIRECT:
                        here = jnp.logical_and(here, jnp.logical_not(self.passes(way)))
                    pl.when(here)(lambda: self.arrival(c, d, way).wait_recv())
        if stage == 0:
            self.started.append(c)

    def finish(self):
        for c in self.started:
            for way in (1, -1):
                for d in self.far(c):
                    pl.when(self.reaches(d, way))(lambda: self.own(c, d, way).wait_send())
                if c not in DIRECT:
                    pl.when(self.passes(way))(lambda: self.passed(c, way).wait_send())


def normed(values, gain):
    mean = jnp.mean(values, axis=-1, keepdims=True)
    centred = values - mean
    spread = jnp.mean(centred * centred, axis=-1, keepdims=True)
    return centred * lax.rsqrt(spread + 1e-06) * gain


def kernel(
    x_ref, halt_ref, gain_ref, qk_ref, w_hbm, wo_hbm, out_ref,
    w, wo, xg, xn, kv, query, counts, flags, hg, pick, place, rest, result, outgoing,
    w_sem, a_send, a_recv, c_send, c_recv, z_send, z_recv, n_send, n_recv, o_send, o_recv, turn,
):
    z = lax.axis_index("dp")
    m = lax.axis_index("mp")
    s = lax.axis_index("section")
    x, y = lax.rem(m, SIDE), m // SIDE
    p = lax.rem(z, GROUP)
    base = z - p

    barrier = pltpu.get_barrier_semaphore()
    peers = [{"dp": base + lax.rem(p + j, GROUP)} for j in (1, 2, 3)]
    neighbours = [
        {"mp": y * SIDE + lax.rem(x + 1, SIDE)},
        {"mp": y * SIDE + lax.rem(x + SIDE - 1, SIDE)},
        {"mp": y * SIDE + lax.rem(x + 2, SIDE)},
        {"mp": lax.rem(y + 1, SIDE) * SIDE + x},
        {"mp": lax.rem(y + 2, SIDE) * SIDE + x},
        {"mp": lax.rem(y + SIDE - 1, SIDE) * SIDE + x},
        {"section": 1 - s},
    ]
    for device in neighbours + peers:
        pl.semaphore_signal(barrier, inc=1, device_id=device, device_id_type=MESH)

    load_w = pltpu.make_async_copy(w_hbm, w, w_sem.at[0])
    load_wo = pltpu.make_async_copy(wo_hbm, wo, w_sem.at[1])
    load_w.start()
    load_wo.start()

    live = jnp.where(halt_ref[...] > s, 1.0, 0.0)
    before = lax.broadcasted_iota(jnp.int32, (TOK, TOK), 0) < lax.broadcasted_iota(jnp.int32, (TOK, TOK), 1)
    rank = jnp.dot(
        jnp.broadcast_to(live, (16, TOK)).astype(BF16),
        jnp.where(before, 1.0, 0.0).astype(BF16),
        preferred_element_type=F32,
    )[0:1]
    count = jnp.sum(live, axis=-1, keepdims=True)
    rank = jnp.where(live > 0.5, rank, -1.0)
    row = lax.broadcasted_iota(jnp.int32, (LIVE, TOK), 0).astype(F32)
    chosen = jnp.broadcast_to(rank, (LIVE, TOK)) == jnp.minimum(row, jnp.broadcast_to(count, (LIVE, TOK)) - 1.0)
    first = jnp.where(chosen, 1.0, 0.0)
    pick[...] = jnp.where(row < jnp.broadcast_to(count, (LIVE, TOK)), first, 0.0)
    compact = jnp.dot(first.astype(BF16), x_ref[...], preferred_element_type=F32).astype(BF16)
    xg[0, 0] = compact
    counts[p] = jnp.broadcast_to(count, (8, 128))

    pl.semaphore_wait(barrier, 10)

    def from_here(b):
        return lax.rem(b // SIDE - y + SIDE, SIDE), lax.rem(b % SIDE - x + SIDE, SIDE)

    ga = Gather(xg, PIECES_A, a_send, a_recv, x, y)
    gc = Gather(hg, PIECES_C, c_send, c_recv, x, y)
    line = Line(kv, z_send, z_recv, z)

    def count_copy(j, ref, device):
        return pltpu.make_async_remote_copy(
            src_ref=ref,
            dst_ref=ref,
            send_sem=n_send.at[j],
            recv_sem=n_recv.at[j],
            device_id=device,
            device_id_type=MESH,
        )

    def project(c):
        low, rows = PARTS[c]
        for at in range(low, low + rows, 64):
            at = slice(at, at + 64)
            total = jnp.zeros((64, 1), F32)
            for b in range(16):
                total += jnp.sum(xg[*from_here(b), at].astype(F32), axis=-1, keepdims=True)
            mean = total * (1.0 / (16 * FEAT))
            square = jnp.zeros((64, 1), F32)
            for b in range(16):
                centred = xg[*from_here(b), at].astype(F32) - mean
                square += jnp.sum(centred * centred, axis=-1, keepdims=True)
            scale = lax.rsqrt(square * (1.0 / (16 * FEAT)) + 1e-06)
            for b in range(16):
                lanes = slice(b * FEAT, (b + 1) * FEAT)
                centred = xg[*from_here(b), at].astype(F32) - mean
                xn[at.start - low : at.stop - low, lanes] = (centred * scale * gain_ref[:, lanes]).astype(BF16)
        if c == 0:
            load_w.wait()
        real = lax.broadcasted_iota(jnp.int32, (rows, HEAD), 0).astype(F32) + low < jnp.broadcast_to(count, (rows, HEAD))
        at = slice(low, low + rows)
        for h in range(HEADS_HERE):
            col = h * 3 * HEAD + HEAD
            total = jnp.zeros((rows, 2 * HEAD), F32)
            for b in range(8):
                depth = slice(b * 2 * FEAT, (b + 1) * 2 * FEAT)
                total += jnp.dot(xn[:rows, depth], w[depth, col : col + 2 * HEAD], preferred_element_type=F32)
            kv[p, at, h * HEAD : (h + 1) * HEAD] = normed(total[:, :HEAD], qk_ref[1, h : h + 1, :]).astype(BF16)
            kv[p, at, WIDE + h * HEAD : WIDE + (h + 1) * HEAD] = jnp.where(real, total[:, HEAD:], 0.0).astype(BF16)

    def ask(c):
        low, rows = PARTS[c]
        total = jnp.zeros((rows, WIDE), F32)
        for b in range(8):
            depth = slice(b * 2 * FEAT, (b + 1) * 2 * FEAT)
            columns = jnp.concatenate([w[depth, :HEAD], w[depth, 3 * HEAD : 4 * HEAD]], axis=1)
            total += jnp.dot(xn[:rows, depth], columns, preferred_element_type=F32)
        for h in range(HEADS_HERE):
            query[h, low : low + rows] = normed(
                total[:, h * HEAD : (h + 1) * HEAD], qk_ref[0, h : h + 1, :]
            ).astype(BF16)

    def attend(c):
        for h in range(HEADS_HERE):
            keys = kv[:, :, h * HEAD : (h + 1) * HEAD].reshape(GROUP * LIVE, HEAD)
            values = kv[:, :, WIDE + h * HEAD : WIDE + (h + 1) * HEAD].reshape(GROUP * LIVE, HEAD)
            scores = (
                lax.dot_general(query[h, c * ROWS : (c + 1) * ROWS], keys, (((1,), (1,)), ((), ())), preferred_element_type=F32) * SCALE
            )
            top = jnp.max(scores, axis=-1, keepdims=True)
            weights = jnp.exp2(scores - top).astype(BF16)
            summed = jnp.dot(
                weights, jnp.concatenate([values, flags[...]], axis=1), preferred_element_type=F32
            )
            heads = (summed[:, :HEAD] / summed[:, HEAD:]).astype(BF16)
            hg[0, 0, c * ROWS : (c + 1) * ROWS, h * HEAD : (h + 1) * HEAD] = heads

    def close(c):
        if c == 0:
            load_wo.wait()
        total = jnp.zeros((ROWS, FEAT), F32)
        for b in range(SIDE):
            heads = jnp.concatenate(
                [hg[*from_here(b * SIDE + i), c * ROWS : (c + 1) * ROWS] for i in range(SIDE)], axis=1
            )
            total += jnp.dot(heads, wo[b * SIDE * WIDE : (b + 1) * SIDE * WIDE, :], preferred_element_type=F32)
        mine = xg[0, 0, c * ROWS : (c + 1) * ROWS].astype(F32)
        result[c * ROWS : (c + 1) * ROWS, :] = (mine + total).astype(BF16)
        low, high = c * ROWS, (c + 1) * ROWS if c < CHUNKS - 1 else TOK
        known = (c + 1) * ROWS
        placed = jnp.dot(place[low:high, :known], result[:known, :], preferred_element_type=F32)
        outgoing[low:high, :] = (rest[low:high, :].astype(F32) + placed).astype(BF16)
        copy = pltpu.make_async_remote_copy(
            src_ref=outgoing.at[pl.ds(low, high - low)],
            dst_ref=out_ref.at[pl.ds(low, high - low)],
            send_sem=o_send.at[c],
            recv_sem=o_recv.at[c],
            device_id={"section": 1 - s},
            device_id_type=MESH,
        )
        copy.start()
        return copy

    copies = []

    def greet():
        for j in (1, 2, 3):
            count_copy(j - 1, counts.at[p], peers[j - 1]).start()

    def prepare():
        place[...] = jnp.transpose(pick[...]).astype(BF16)
        rest[...] = (
            x_ref[...].astype(F32) - jnp.dot(place[...], compact, preferred_element_type=F32)
        ).astype(BF16)
        for j in (1, 2, 3):
            count_copy(j - 1, counts.at[lax.rem(p + GROUP - j, GROUP)], peers[j - 1]).wait_recv()
        place_of = lax.broadcasted_iota(jnp.int32, (LIVE, HEAD), 0).astype(F32)
        for q in range(GROUP):
            flags[q * LIVE : (q + 1) * LIVE, :] = jnp.where(
                place_of < jnp.broadcast_to(counts[q, 0:1, :], (LIVE, HEAD)), 1.0, 0.0
            ).astype(BF16)

    def gate():
        pl.when(s == 1)(lambda: pl.semaphore_wait(turn, 1))

    def open_gate():
        @pl.when(s == 0)
        def _():
            pl.semaphore_signal(turn, inc=1, device_id={"section": 1 - s}, device_id_type=MESH)

    steps = {
        "a": ga.step, "c": gc.step, "z": line.step, "project": project, "ask": ask, "attend": attend,
        "close": lambda c: copies.append(close(c)), "greet": greet, "prepare": prepare,
        "gate": gate, "open": open_gate,
    }
    for name, *at in ORDER:
        steps[name](*at)

    for j in (1, 2, 3):
        count_copy(j - 1, counts.at[p], peers[j - 1]).wait_send()
    ga.finish()
    gc.finish()
    line.finish()
    for copy in copies:
        copy.wait()


def body(acts, halting, norm_gain, qkv_weight, qk_gain, out_weight):
    vmem = pl.BlockSpec(memory_space=pltpu.VMEM)
    anywhere = pl.BlockSpec(memory_space=pl.ANY)
    out = pl.pallas_call(
        kernel,
        out_shape=jax.ShapeDtypeStruct((TOK, FEAT), BF16),
        in_specs=[vmem, vmem, vmem, vmem, anywhere, anywhere],
        out_specs=anywhere,
        scratch_shapes=[
            pltpu.VMEM((16 * FEAT, COLS), BF16),
            pltpu.VMEM((16 * WIDE, FEAT), BF16),
            pltpu.VMEM((SIDE, SIDE, LIVE, FEAT), BF16),
            pltpu.VMEM((ROWS, 16 * FEAT), BF16),
            pltpu.VMEM((GROUP, LIVE, 2 * WIDE), BF16),
            pltpu.VMEM((HEADS_HERE, LIVE, HEAD), BF16),
            pltpu.VMEM((GROUP, 8, 128), F32),
            pltpu.VMEM((GROUP * LIVE, HEAD), BF16),
            pltpu.VMEM((SIDE, SIDE, LIVE, WIDE), BF16),
            pltpu.VMEM((LIVE, TOK), F32),
            pltpu.VMEM((TOK, LIVE), BF16),
            pltpu.VMEM((TOK, FEAT), BF16),
            pltpu.VMEM((LIVE, FEAT), BF16),
            pltpu.VMEM((TOK, FEAT), BF16),
            pltpu.SemaphoreType.DMA((2,)),
            pltpu.SemaphoreType.DMA((len(PIECES_A) * 9,)),
            pltpu.SemaphoreType.DMA((len(PIECES_A) * 9,)),
            pltpu.SemaphoreType.DMA((len(PIECES_C) * 9,)),
            pltpu.SemaphoreType.DMA((len(PIECES_C) * 9,)),
            pltpu.SemaphoreType.DMA((len(PARTS) * 6,)),
            pltpu.SemaphoreType.DMA((len(PARTS) * 6,)),
            pltpu.SemaphoreType.DMA((3,)),
            pltpu.SemaphoreType.DMA((3,)),
            pltpu.SemaphoreType.DMA((CHUNKS,)),
            pltpu.SemaphoreType.DMA((CHUNKS,)),
            pltpu.SemaphoreType.REGULAR,
        ],
        compiler_params=pltpu.CompilerParams(
            collective_id=0, has_side_effects=True, vmem_limit_bytes=56 * 1024 * 1024
        ),
    )(acts[0], halting, norm_gain, qk_gain[0], qkv_weight[0], out_weight[0])
    return out[None]


def solution(mesh):
    return jax.shard_map(
        body,
        mesh=mesh,
        in_specs=(
            P("section", "dp", "mp"),
            P("section", "dp"),
            P("section", None),
            P("section", None, "mp"),
            P("section", None, "mp", None),
            P("section", None, "mp"),
        ),
        out_specs=P("section", "dp", "mp"),
        check_vma=False,
    )
```
